512 devices in a mesh: views: 8 (over x, z_hi), depth: 64 (over y, z_lo, core).
Axes of the slice: x: 4, y: 8, z: 8 (z_hi: 2, z_lo: 4; z = z_hi * 4 + z_lo), core: 2. Of those that a mesh axis runs over, the one named last changes fastest.
Arguments:
- concentration: float32 [8, 1, 2048, 1024], P(None, None, 'depth'), may hold values from 0 to 1
- shear_index: int32 [16, 2048, 1024], P('views', 'depth'), may hold values from 0 to 1022, as said below
- shear_weight: float32 [16, 2048, 1024], P('views', 'depth'), may hold values from 0 to 1
- attenuation: float32 [4, 8], replicated, may hold values from 2.4414063e-05 to 0.00048828125
- yields: float32 [8], replicated, may hold values from 0.5 to 2
- line_energy: int32 [8], replicated, may hold values from 0 to 2
- measured: float32 [16, 8, 1, 1024], P('views'), may hold values from -4 to 4
Outputs:
- gradient: float32 [8, 1, 2048, 1024], P(None, None, 'depth')
- signal: float32 [16, 8, 1, 1024], P('views')
The draws below stay inside these ranges and needn't reach their ends.
Inputs may be any that keep to these rules, and one draw needn't show every extreme that they name: shear_index[v, d, t] is t plus a shift of that view and depth cell, the shift between -128 and 128, clipped to the grid.
All inputs are finite; a program needn't handle non-finite values.
Results may differ from the reference program's by a relative error of at most 0.0001.
Values sent between devices are 32-bit elements; how exact they have to be, the bound alone decides.
A program may use at most 64 MiB of HBM per device.

```python
import math
import jax
import jax.numpy as jnp
from jax import lax

ELEMENTS = 8
EMISSIONS = 3
ROWS = 1
DSLAB = 32
WIDTH = 1024
VIEWS = 16
NDEPTH = 2048
N_DEPTH = 64


def draw_shear_index(key, part):
    key = jax.random.fold_in(key, 11)
    shifts = jax.random.randint(key, (VIEWS, NDEPTH), -(WIDTH // 8), WIDTH // 8 + 1).astype(jnp.int32)
    shifts = shifts.at[0, 0].set(0)
    positions = jnp.arange(WIDTH, dtype=jnp.int32)
    return jnp.clip(positions[None, None, :] + shifts[:, :, None], 0, WIDTH - 2).astype(jnp.int32)


def set_ends(values, stream_key, least, top_value):
    longest = values.shape.index(max(values.shape))
    spots = []
    for shift in (0, 1):
        where = [jax.random.randint(jax.random.fold_in(stream_key, axis), (), 0, length) for axis, length in enumerate(values.shape)]
        where[longest] = (where[longest] + shift) % values.shape[longest]
        spots.append(tuple(where))
    return values.at[spots[0]].set(least).at[spots[1]].set(top_value)


def block_levels(rng, dims, cuts, least, top_value):
    def one(axis_at, parts):
        draws = jax.random.uniform(jax.random.fold_in(jax.random.fold_in(rng, 6), axis_at), (parts,), jnp.float32, least / len(cuts), top_value / len(cuts))
        return jnp.repeat(jnp.exp(draws), dims[axis_at] // parts).reshape((-1,) + (1,) * (len(dims) - axis_at - 1))

    loudness = one(*cuts[0])
    for cut in cuts[1:]:
        loudness = loudness * one(*cut)
    return loudness


def noise(rng, dims, deviation, limit, cuts=(), kind=jnp.bfloat16):
    result = deviation * jax.random.normal(rng, dims, jnp.float32)
    if cuts:
        result = result * block_levels(rng, dims, cuts, -0.22, 0.18)
    return jnp.clip(result, -limit, limit).astype(kind)


def setup_inputs(seed: int = 0) -> dict:
    keys = jax.random.split(jax.random.key(seed), 8)
    return {
        "concentration": jnp.clip(1.0 * jax.random.uniform(keys[0], (ELEMENTS, ROWS, NDEPTH, WIDTH), jnp.float32) ** block_levels(keys[0], (ELEMENTS, ROWS, NDEPTH, WIDTH), ((2, 64),), -0.2, 0.2), 0.0, 1.0),
        "shear_index": draw_shear_index(jax.random.fold_in(keys[7], 71), 0),
        "shear_weight": jnp.clip(1.0 * jax.random.uniform(keys[2], (VIEWS, NDEPTH, WIDTH), jnp.float32) ** block_levels(keys[2], (VIEWS, NDEPTH, WIDTH), ((0, 8), (1, 64)), -0.2, 0.2), 0.0, 1.0),
        "attenuation": jnp.clip(jnp.exp(jax.random.uniform(keys[3], (EMISSIONS + 1, ELEMENTS), jnp.float32, math.log(2.441406286379788e-05), math.log(0.00048828125))), 2.441406286379788e-05, 0.00048828125),
        "yields": jnp.clip(jnp.exp(jax.random.uniform(keys[4], (ELEMENTS,), jnp.float32, math.log(0.5), math.log(2.0))), 0.5, 2.0),
        "line_energy": set_ends(jax.random.randint(keys[5], (ELEMENTS,), 0, EMISSIONS), jax.random.fold_in(keys[5], 1), 0, EMISSIONS - 1).astype(jnp.int32),
        "measured": noise(keys[6], (VIEWS, ELEMENTS, ROWS, WIDTH), 0.5, 4.0, ((0, 8),), jnp.float32),
    }


def reference(concentration, shear_index, shear_weight, attenuation, yields, line_energy, measured):
    depth_total = DSLAB * N_DEPTH
    highest = lax.Precision.HIGHEST
    selector = (line_energy[:, None] == jnp.arange(EMISSIONS, dtype=jnp.int32)[None, :]).astype(jnp.float32)
    cells = ELEMENTS * ROWS * depth_total * WIDTH
    offsets = (jnp.arange(ELEMENTS * ROWS * depth_total, dtype=jnp.int32) * WIDTH).reshape(ELEMENTS, ROWS, depth_total, 1)

    def one_view(carry, inputs):
        index_view, weight_view, measured_view = inputs
        index_full = jnp.broadcast_to(index_view[None, None], concentration.shape)
        left = jnp.take_along_axis(concentration, index_full, axis=3)
        right = jnp.take_along_axis(concentration, index_full + 1, axis=3)
        field = left * (1.0 - weight_view) + right * weight_view
        absorb = jnp.einsum('ke,erdw->krdw', attenuation, field, precision=highest)
        running = jnp.cumsum(absorb, axis=2)
        incident = jnp.exp(-(running[0] - absorb[0]))
        leaving = jnp.exp(-(running[1:, :, -1:] - running[1:]))
        leaving_line = jnp.einsum('lk,krdw->lrdw', selector, leaving, precision=highest)
        emitted = yields[:, None, None, None] * field * incident[None] * leaving_line / depth_total
        signal_view = jnp.sum(emitted, axis=2)
        misfit = signal_view - measured_view
        weighted = misfit[:, :, None, :] * emitted
        backward = jnp.sum(weighted, axis=0)
        back_run = jnp.cumsum(backward, axis=1)
        suffix = back_run[:, -1:] - back_run
        forward = jnp.einsum('lk,lrdw->krdw', selector, weighted, precision=highest)
        prefix = jnp.cumsum(forward, axis=2) - forward
        direct = misfit[:, :, None, :] * yields[:, None, None, None] * incident[None] * leaving_line
        view_grad = direct - depth_total * (attenuation[0][:, None, None, None] * suffix[None]
                                            + jnp.einsum('ke,krdw->erdw', attenuation[1:], prefix, precision=highest))
        spot = (offsets + index_full).reshape(-1)
        values = jnp.concatenate([(view_grad * (1.0 - weight_view)).reshape(-1), (view_grad * weight_view).reshape(-1)])
        places = jnp.concatenate([spot, spot + 1])
        local = jax.ops.segment_sum(values, places, num_segments=cells).reshape(concentration.shape)
        return carry + local, signal_view

    start = jnp.zeros(concentration.shape, jnp.float32)
    gradient, signal = lax.scan(one_view, start, (shear_index, shear_weight, measured))
    return gradient, signal
```

```python
import functools

import jax
import jax.numpy as jnp
from jax import lax
from jax.experimental import pallas as pl
from jax.experimental.pallas import tpu as pltpu
from jax.sharding import PartitionSpec as P

LANES = 128
TILE = 8
STEP = 256
MESH = pl.DeviceIdType.MESH
F32 = jnp.float32
BF16 = jnp.bfloat16


def split(value):
    high = value.astype(BF16)
    low = (value - high.astype(F32)).astype(BF16)
    return high, low


def dot3(high_ref, low_ref, right):
    right_high, right_low = split(right)
    high = high_ref[...]
    result = jnp.dot(high, right_high, preferred_element_type=F32)
    result += jnp.dot(high, right_low, preferred_element_type=F32)
    return result + jnp.dot(low_ref[...], right_high, preferred_element_type=F32)


def kernel(
    sizes,
    starts,
    att,
    yields,
    line,
    conc,
    weight,
    measured,
    grad,
    signal,
    mat_high,
    mat_low,
    adj_high,
    adj_low,
    pad_left,
    pad_step,
    field,
    decay,
    spread_left,
    spread_right,
    corr,
    slab,
    group,
    local_scale,
    local_part,
    group_send,
    group_recv,
    group_scale,
    back,
    seeds,
    total_send,
    part,
    from_x,
    z_out,
    from_z,
    send1,
    recv1,
    send2,
    recv2,
    send3,
    recv3,
    send4,
    recv4,
    send5,
    recv5,
    send6,
    recv6,
    send7,
    recv7,
    send8,
):
    nx, nz, ny, nc = sizes
    views, depth, width = weight.shape
    blocks = width // LANES
    wide = views * width // nc
    per_view = width // wide
    depth_total = depth * ny * nc
    vi, di = lax.axis_index("views"), lax.axis_index("depth")
    x, zh = vi // nz, vi % nz
    y, c = di // nc, di % nc

    def in_group(k):
        return y * nc + k

    def in_y(k):
        return k * nc + c

    def in_x(k):
        return k * nz + zh

    def in_z(k):
        return x * nz + k

    barrier = pltpu.get_barrier_semaphore()
    greeted = 0
    for k in range(1, nc):
        pl.semaphore_signal(barrier, inc=1, device_id={"depth": in_group((c + k) % nc)}, device_id_type=MESH)
        greeted += 1
    for k in range(1, ny):
        pl.semaphore_signal(barrier, inc=1, device_id={"depth": in_y((y + k) % ny)}, device_id_type=MESH)
        greeted += 1
    for k in range(1, nx):
        pl.semaphore_signal(barrier, inc=1, device_id={"views": in_x((x + k) % nx)}, device_id_type=MESH)
        greeted += 1
    for k in range(1, nz):
        pl.semaphore_signal(barrier, inc=1, device_id={"views": in_z((zh + k) % nz)}, device_id_type=MESH)
        greeted += 1

    rows16 = lax.broadcasted_iota(jnp.int32, (2 * TILE, depth * TILE), 0)
    cols16 = lax.broadcasted_iota(jnp.int32, (2 * TILE, depth * TILE), 1)
    row_item, col_item, col_depth = rows16 & (TILE - 1), cols16 & (TILE - 1), cols16 // TILE

    def spread(item, values):
        result = jnp.full(item.shape, values[0])
        for i in range(1, TILE):
            result = jnp.where(item == i, values[i], result)
        return result

    att_col = [spread(col_item, [att[k, e] for e in range(TILE)]) for k in range(4)]
    att_row = [spread(row_item, [att[k, e] for e in range(TILE)]) for k in range(4)]
    line_col = spread(col_item, [line[e] for e in range(TILE)])
    line_row = spread(row_item, [line[e] for e in range(TILE)])

    def pick(which, options):
        return jnp.where(which == 0, options[0], jnp.where(which == 1, options[1], options[2]))

    forward_out = pick(line_row, att_col[1:])
    adjoint_out = pick(line_col, att_row[1:])
    for i in range(depth // 2):
        here = rows16 // TILE + 2 * i
        rows = pl.ds(2 * TILE * i, 2 * TILE)
        mat = jnp.where(col_depth < here, att_col[0], jnp.where(col_depth > here, forward_out, 0.0))
        mat_high[rows, :], mat_low[rows, :] = split(mat)
        adj = jnp.where(col_depth > here, att_row[0], jnp.where(col_depth < here, adjoint_out, 0.0))
        adj_high[rows, :], adj_low[rows, :] = split(adj)
    att_tile = [value[:TILE, :LANES] for value in att_row]
    line_tile = line_row[:TILE, :LANES]
    yield_tile = spread(row_item[:TILE, :LANES], [yields[e] for e in range(TILE)])

    def over(tile, columns):
        return jnp.concatenate([tile] * (columns // LANES), axis=1)

    lane = lax.broadcasted_iota(jnp.int32, (TILE, LANES), 1)
    sub = lax.broadcasted_iota(jnp.int32, (TILE, LANES), 0)

    def turn_rows(i, carry):
        at = pl.ds(pl.multiple_of(i * TILE, TILE), TILE)
        for j in range(blocks):
            columns = slice(j * LANES, (j + 1) * LANES)
            part[at, :, columns] = jnp.transpose(conc[:, at, columns], (1, 0, 2))
        return carry

    lax.fori_loop(0, depth // TILE, turn_rows, 0)

    def pad_row(d, carry):
        x_blocks = [part[d, :, j * LANES : (j + 1) * LANES] for j in range(blocks)]
        turned = [pltpu.roll(block, LANES - 1, 1) for block in x_blocks]

        def lane_of(block, at):
            return jnp.broadcast_to(block[:, at : at + 1], (TILE, LANES))

        first, second = lane_of(x_blocks[0], 0), lane_of(x_blocks[0], 1)
        before_last, last = lane_of(x_blocks[-1], LANES - 2), lane_of(x_blocks[-1], LANES - 1)
        pad_left[d, 0] = first
        pad_step[d, 0] = second - first
        for j in range(blocks):
            if j < blocks - 1:
                left = x_blocks[j]
                right = jnp.where(lane == LANES - 1, turned[j + 1], turned[j])
            else:
                left = jnp.where(lane == LANES - 1, before_last, x_blocks[j])
                right = jnp.where(lane == LANES - 1, last, turned[j])
            pad_left[d, j + 1] = left
            pad_step[d, j + 1] = right - left
        for j in (blocks + 1, blocks + 2):
            pad_left[d, j] = before_last
            pad_step[d, j] = last - before_last
        return carry

    lax.fori_loop(0, depth, pad_row, 0, unroll=2)

    for v in range(views):

        def take_row(d, row, shares, sums):
            start = starts[v, d]
            block, rest = start >> 7, start & (LANES - 1)
            turn = (LANES - rest) & (LANES - 1)
            left = pltpu.roll(pad_left[d, pl.ds(block, blocks + 1)], turn, 2)
            step = pltpu.roll(pad_step[d, pl.ds(block, blocks + 1)], turn, 2)
            whole = lane < LANES - rest
            new = []
            for j in range(blocks):
                at = pl.ds(j * LANES, LANES)
                share = jnp.broadcast_to(shares[row : row + 1, j * LANES : (j + 1) * LANES], (TILE, LANES))
                value = jnp.where(whole, left[j], left[j + 1]) + share * jnp.where(whole, step[j], step[j + 1])
                field[v, pl.ds(pl.multiple_of(d * TILE, TILE), TILE), at] = value
                new.append(sums[j] + value)
            return tuple(new)

        def take_rows(i, sums):
            base = pl.multiple_of(i * TILE, TILE)
            shares = weight[v, pl.ds(base, TILE), :]
            for row in range(TILE):
                sums = take_row(base + row, row, shares, sums)
            return sums

        zero = jnp.zeros((TILE, LANES), F32)
        sums = lax.fori_loop(0, depth // TILE, take_rows, (zero,) * blocks)
        for j in range(blocks):
            chunk, offset = divmod((v * width + j * LANES), wide)
            absorbed = jnp.zeros((TILE, LANES), F32)
            for k in range(4):
                level = jnp.sum(att_tile[k] * sums[j], axis=0, keepdims=True)
                absorbed = jnp.where(sub == k, jnp.broadcast_to(level, (TILE, LANES)), absorbed)
            slab[chunk, TILE:, offset : offset + LANES] = absorbed

    pl.semaphore_wait(barrier, greeted)

    def to_group(k):
        return pltpu.make_async_remote_copy(
            src_ref=slab.at[k],
            dst_ref=group.at[c],
            send_sem=send1.at[k],
            recv_sem=recv1.at[c],
            device_id={"depth": in_group(k)},
            device_id_type=MESH,
        )

    def emit(i, carry):
        chunk = (c + 1 + i) % nc
        v, base = chunk // per_view, (chunk % per_view) * wide
        for part_at in range(0, wide, STEP):
            at = pl.ds(pl.multiple_of(base + part_at, STEP), STEP)
            values = field[v, :, at]
            value = jnp.exp(-dot3(mat_high, mat_low, values))
            decay[v, :, at] = value
            value = (value * values).reshape(depth, TILE, STEP)
            slab[chunk, :TILE, part_at : part_at + STEP] = jnp.sum(value, axis=0) * over(yield_tile, STEP)

        @pl.when(chunk != c)
        def _():
            to_group(chunk).start()

        return carry

    lax.fori_loop(0, nc, emit, 0)
    group[c] = slab[c]

    def from_group(k):
        return pltpu.make_async_remote_copy(
            src_ref=slab.at[k],
            dst_ref=group.at[k],
            send_sem=send1.at[k],
            recv_sem=recv1.at[k],
            device_id={"depth": in_group(k)},
            device_id_type=MESH,
        )

    for k in range(1, nc):
        from_group((c + k) % nc).wait_recv()

    line_wide = over(line_tile, wide)
    att_wide = [over(tile, wide) for tile in att_tile]

    def scales(ref, count):
        first, later = [], []
        for j in range(count):
            levels = [jnp.broadcast_to(ref[j, TILE + k : TILE + k + 1, :], (TILE, wide)) for k in range(4)]
            first.append(levels[0])
            later.append(pick(line_wide, levels[1:]))
        after = [None] * count
        run = jnp.zeros((TILE, wide), F32)
        for j in reversed(range(count)):
            after[j] = run
            run = run + later[j]
        result = []
        run = jnp.zeros((TILE, wide), F32)
        for j in range(count):
            result.append(jnp.exp(-(run + after[j])))
            run = run + first[j]
        return result

    emitted_sum = jnp.zeros((TILE, wide), F32)
    absorbed_sum = jnp.zeros((TILE, wide), F32)
    for j, scale in enumerate(scales(group, nc)):
        piece = group[j, :TILE, :] * scale
        local_scale[j] = scale
        local_part[j] = piece
        emitted_sum += piece
        absorbed_sum += group[j, TILE:, :]
    group_send[:TILE, :] = emitted_sum
    group_send[TILE:, :] = absorbed_sum

    def y_copy(peer, slot):
        return pltpu.make_async_remote_copy(
            src_ref=group_send,
            dst_ref=group_recv.at[slot],
            send_sem=send2.at[peer],
            recv_sem=recv2.at[slot],
            device_id={"depth": in_y(peer)},
            device_id_type=MESH,
        )

    for k in range(1, ny):
        y_copy((y + k) % ny, y).start()
    group_recv[y] = group_send[...]
    for k in range(1, ny):
        y_copy((y + k) % ny, (y + k) % ny).wait_recv()

    total = jnp.zeros((TILE, wide), F32)
    prior = jnp.zeros((TILE, wide), F32)
    following = jnp.zeros((TILE, wide), F32)
    for j, scale in enumerate(scales(group_recv, ny)):
        piece = group_recv[j, :TILE, :] * scale
        group_scale[j] = scale
        total += piece
        prior += jnp.where(j < y, piece, 0.0)
        following += jnp.where(j > y, piece, 0.0)
    own_view, own_base = c // per_view, pl.multiple_of((c % per_view) * wide, LANES)
    own_at = pl.ds(own_base, wide)
    counts = total * (1.0 / depth_total)
    misfit = counts - measured[own_view, :, own_at]
    here_scale = group_scale[y]
    run = following
    for j in reversed(range(nc)):
        level = jnp.sum(misfit * run, axis=0, keepdims=True)
        back[j, TILE:, :] = att_wide[0] * level
        run = run + local_part[j] * here_scale
    run = prior
    yield_wide = over(yield_tile, wide)
    for j in range(nc):
        back[j, :TILE, :] = misfit * yield_wide * local_scale[j] * here_scale
        mixed = misfit * run
        extra = jnp.zeros((TILE, wide), F32)
        for k in range(3):
            level = jnp.sum(jnp.where(line_wide == k, mixed, 0.0), axis=0, keepdims=True)
            extra += att_wide[k + 1] * level
        back[j, TILE:, :] += extra
        run = run + local_part[j] * here_scale

    def seed_copy(peer, slot):
        return pltpu.make_async_remote_copy(
            src_ref=back.at[peer],
            dst_ref=seeds.at[slot],
            send_sem=send3.at[peer],
            recv_sem=recv3.at[slot],
            device_id={"depth": in_group(peer)},
            device_id_type=MESH,
        )

    def total_copy(peer, slot):
        at = pl.ds(pl.multiple_of((slot % per_view) * wide, LANES), wide)
        return pltpu.make_async_remote_copy(
            src_ref=total_send,
            dst_ref=signal.at[slot // per_view, :, at],
            send_sem=send4.at[peer],
            recv_sem=recv4.at[slot],
            device_id={"depth": in_group(peer)},
            device_id_type=MESH,
        )

    for k in range(1, nc):
        seed_copy((c + k) % nc, c).start()
    seeds[c] = back[c]
    total_send[...] = counts
    signal[own_view, :, own_at] = counts
    for k in range(1, nc):
        total_copy((c + k) % nc, c).start()

    def clear(d, carry):
        zeros = jnp.zeros((3, TILE, LANES), F32)
        for v in range(views):
            spread_left[v, d, 0:3] = zeros
            spread_right[v, d, 0:3] = zeros
            spread_left[v, d, 3 + blocks : 5 + blocks] = zeros[:2]
            spread_right[v, d, 3 + blocks : 5 + blocks] = zeros[:2]
        return carry

    lax.fori_loop(0, depth, clear, 0)

    for k in range(1, nc):
        seed_copy((c + k) % nc, (c + k) % nc).wait_recv()

    def adjoint(chunk, carry):
        v, base = chunk // per_view, (chunk % per_view) * wide
        for part_at in range(0, wide, STEP):
            start = pl.multiple_of(base + part_at, STEP)
            at = pl.ds(start, STEP)
            factor = seeds[chunk, :TILE, part_at : part_at + STEP]
            constant = seeds[chunk, TILE:, part_at : part_at + STEP]
            direct = decay[v, :, at].reshape(depth, TILE, STEP) * factor[None]
            mixed = direct.reshape(depth * TILE, STEP) * field[v, :, at]
            corr[...] = dot3(adj_high, adj_low, mixed)

            def some(i, inner):
                shares = weight[v, pl.ds(pl.multiple_of(i * TILE, TILE), TILE), at]
                for row in range(TILE):
                    d = i * TILE + row
                    rows = pl.ds(pl.multiple_of(d * TILE, TILE), TILE)
                    value = decay[v, rows, at] * factor - corr[rows, :] - constant
                    right = value * jnp.broadcast_to(shares[row : row + 1], (TILE, STEP))
                    left = value - right
                    for j in range(STEP // LANES):
                        to = 3 + start // LANES + j
                        spread_left[v, d, to] = left[:, j * LANES : (j + 1) * LANES]
                        spread_right[v, d, to] = right[:, j * LANES : (j + 1) * LANES]
                return inner

            lax.fori_loop(0, depth // TILE, some, 0)
        return carry

    lax.fori_loop(0, nc, adjoint, 0)

    share_x = depth // nx
    share_z = share_x // nz

    def x_copy(peer, slot):
        return pltpu.make_async_remote_copy(
            src_ref=part.at[pl.ds(peer * share_x, share_x)],
            dst_ref=from_x.at[slot],
            send_sem=send5.at[peer],
            recv_sem=recv5.at[slot],
            device_id={"views": in_x(peer)},
            device_id_type=MESH,
        )

    def place(i, carry):
        peer = (x + 1 + i) % nx

        def place_row(r, inner):
            d = peer * share_x + r
            lefts = [None] * (blocks + 2)
            rights = [None] * (blocks + 2)
            for v in range(views):
                start = starts[v, d]
                block, rest = start >> 7, start & (LANES - 1)
                for ref, sums in ((spread_left, lefts), (spread_right, rights)):
                    turned = pltpu.roll(ref[v, d, pl.ds(2 - block, blocks + 3)], rest, 2)
                    for j in range(blocks + 2):
                        value = jnp.where(lane >= rest, turned[j + 1], turned[j])
                        sums[j] = value if v == 0 else sums[j] + value

            def total_of(value):
                return jnp.sum(value, axis=1, keepdims=True)

            low_left, low_right = total_of(lefts[0]), total_of(rights[0])
            top = lane == LANES - 1
            high_left = total_of(lefts[-1] + jnp.where(top, lefts[-2], 0.0))
            high_right = total_of(rights[-1])
            shifted = [pltpu.roll(rights[j + 1], 1, 1) for j in range(blocks)]
            for j in range(blocks):
                left = lefts[j + 1]
                if j == 0:
                    right = jnp.where(lane == 0, 0.0, shifted[0])
                    left = left + jnp.where(lane == 0, low_left, 0.0) + jnp.where(lane == 1, low_right, 0.0)
                else:
                    right = jnp.where(lane == 0, shifted[j - 1], shifted[j])
                if j == blocks - 1:
                    left = jnp.where(top, high_right + rights[-2], left)
                    left = left + jnp.where(lane == LANES - 2, high_left, 0.0)
                part[d, :, j * LANES : (j + 1) * LANES] = left + right
            return inner

        lax.fori_loop(0, share_x, place_row, 0)

        @pl.when(peer != x)
        def _():
            x_copy(peer, x).start()

        return carry

    lax.fori_loop(0, nx, place, 0)

    for k in range(1, nx):
        x_copy((x + k) % nx, (x + k) % nx).wait_recv()

    def reduced(r):
        value = part[x * share_x + r]
        for k in range(1, nx):
            value = value + from_x[(x + k) % nx, r]
        return value

    def z_copy(peer, slot):
        return pltpu.make_async_remote_copy(
            src_ref=z_out.at[peer],
            dst_ref=from_z.at[slot],
            send_sem=send6.at[peer],
            recv_sem=recv6.at[slot],
            device_id={"views": in_z(peer)},
            device_id_type=MESH,
        )

    for k in range(1, nz):
        peer = (zh + k) % nz

        def gather_z(r, carry):
            z_out[peer, r] = reduced(peer * share_z + r)
            return carry

        lax.fori_loop(0, share_z, gather_z, 0)
        z_copy(peer, zh).start()

    def own(r, carry):
        z_out[zh, r] = reduced(zh * share_z + r)
        return carry

    lax.fori_loop(0, share_z, own, 0)
    for k in range(1, nz):
        z_copy((zh + k) % nz, (zh + k) % nz).wait_recv()

    def finish(r, carry):
        value = z_out[zh, r]
        for k in range(1, nz):
            value = value + from_z[(zh + k) % nz, r]
        grad[x * share_x + zh * share_z + r] = value
        return carry

    lax.fori_loop(0, share_z, finish, 0)

    def piece(px, pz):
        return grad.at[pl.ds(px * share_x + pz * share_z, share_z)]

    def give_x(peer, px, pz):
        return pltpu.make_async_remote_copy(
            src_ref=piece(px, pz),
            dst_ref=piece(px, pz),
            send_sem=send7.at[peer, pz],
            recv_sem=recv7.at[px, pz],
            device_id={"views": in_x(peer)},
            device_id_type=MESH,
        )

    def give_z(peer, px, pz):
        return pltpu.make_async_remote_copy(
            src_ref=piece(px, pz),
            dst_ref=piece(px, pz),
            send_sem=send8.at[peer],
            recv_sem=recv7.at[px, pz],
            device_id={"views": in_z(peer)},
            device_id_type=MESH,
        )

    for k in range(1, nz):
        give_z((zh + k) % nz, x, zh).start()
    for k in range(1, nx):
        give_x((x + k) % nx, x, zh).start()
    for k in range(1, nz):
        pz = (zh + k) % nz
        give_z(pz, x, pz).wait_recv()
        for m in range(1, nx):
            give_x((x + m) % nx, x, pz).start()
    for k in range(nz):
        pz = (zh + k) % nz
        for m in range(1, nx):
            give_x((x + m) % nx, (x + m) % nx, pz).wait_recv()
    for k in range(1, nc):
        total_copy((c + k) % nc, (c + k) % nc).wait_recv()

    for k in range(1, nc):
        peer = (c + k) % nc
        to_group(peer).wait_send()
        seed_copy(peer, c).wait_send()
        total_copy(peer, c).wait_send()
    for k in range(1, ny):
        y_copy((y + k) % ny, y).wait_send()
    for k in range(1, nx):
        peer = (x + k) % nx
        x_copy(peer, x).wait_send()
        for pz in range(nz):
            give_x(peer, x, pz).wait_send()
    for k in range(1, nz):
        peer = (zh + k) % nz
        z_copy(peer, zh).wait_send()
        give_z(peer, x, zh).wait_send()


def body(sizes, concentration, shear_index, shear_weight, attenuation, yields, line_energy, measured):
    elements, rows, depth, width = concentration.shape
    views = shear_index.shape[0]
    nx, nz, ny, nc = sizes
    wide = views * width // nc
    blocks = width // LANES
    starts = shear_index[:, :, width // 2] - (width // 2 - LANES)
    smem = pl.BlockSpec(memory_space=pltpu.SMEM)
    vmem = pl.BlockSpec(memory_space=pltpu.VMEM)
    full = depth * elements

    def buf(*shape):
        return pltpu.VMEM(shape, F32)

    def sems(*shape):
        return pltpu.SemaphoreType.DMA(shape)

    gradient, signal = pl.pallas_call(
        functools.partial(kernel, sizes),
        out_shape=(
            jax.ShapeDtypeStruct((depth, elements, width), F32),
            jax.ShapeDtypeStruct((views, elements, width), F32),
        ),
        in_specs=[smem] * 4 + [vmem] * 3,
        out_specs=(vmem, vmem),
        scratch_shapes=[pltpu.VMEM((full, full), BF16)] * 4
        + [buf(depth, blocks + 3, elements, LANES)] * 2
        + [buf(views, full, width)] * 2
        + [buf(views, depth, blocks + 5, elements, LANES)] * 2
        + [
            buf(full, STEP),
            buf(nc, 2 * elements, wide),
            buf(nc, 2 * elements, wide),
            buf(nc, elements, wide),
            buf(nc, elements, wide),
            buf(2 * elements, wide),
            buf(ny, 2 * elements, wide),
            buf(ny, elements, wide),
            buf(nc, 2 * elements, wide),
            buf(nc, 2 * elements, wide),
            buf(elements, wide),
            buf(depth, elements, width),
            buf(nx, depth // nx, elements, width),
            buf(nz, depth // nx // nz, elements, width),
            buf(nz, depth // nx // nz, elements, width),
        ]
        + [sems(nc)] * 2
        + [sems(ny)] * 2
        + [sems(nc)] * 4
        + [sems(nx)] * 2
        + [sems(nz)] * 2
        + [sems(nx, nz)] * 2
        + [sems(nz)],
        compiler_params=pltpu.CompilerParams(
            collective_id=0, has_side_effects=True, vmem_limit_bytes=44 * 1024 * 1024
        ),
    )(
        starts,
        attenuation,
        yields,
        line_energy,
        concentration.reshape(elements, depth, width),
        shear_weight,
        measured.reshape(views, elements, width),
    )
    gradient = jnp.transpose(gradient, (1, 0, 2)).reshape(elements, rows, depth, width)
    return gradient, signal.reshape(views, elements, rows, width)


SIZES = {(8, 64): (4, 2, 8, 8)}


def solution(mesh):
    sizes = SIZES[mesh.shape["views"], mesh.shape["depth"]]
    return jax.shard_map(
        functools.partial(body, sizes),
        mesh=mesh,
        in_specs=(
            P(None, None, "depth", None),
            P("views", "depth", None),
            P("views", "depth", None),
            P(),
            P(),
            P(),
            P("views", None, None, None),
        ),
        out_specs=(P(None, None, "depth", None), P("views", None, None, None)),
        check_vma=False,
    )
```

```python
import functools

import jax
import jax.numpy as jnp
from jax import lax
from jax.experimental import pallas as pl
from jax.experimental.pallas import tpu as pltpu
from jax.sharding import PartitionSpec as P

LANES = 128
TILE = 8
STEP = 256
PAIR = 2
MESH = pl.DeviceIdType.MESH
F32 = jnp.float32
BF16 = jnp.bfloat16


def split(value):
    high = value.astype(BF16)
    low = (value - high.astype(F32)).astype(BF16)
    return high, low


def dot3(high_ref, low_ref, right):
    right_high, right_low = split(right)
    high = high_ref[...]
    result = jnp.dot(high, right_high, preferred_element_type=F32)
    result += jnp.dot(high, right_low, preferred_element_type=F32)
    return result + jnp.dot(low_ref[...], right_high, preferred_element_type=F32)


def kernel(
    sizes,
    index_in,
    att_in,
    yields_in,
    line_in,
    conc_in,
    weight_in,
    measured_in,
    grad,
    signal,
    shifts,
    att,
    yields,
    line,
    conc,
    weight,
    measured,
    fetched,
    mat_high,
    mat_low,
    adj_high,
    adj_low,
    pad_left,
    pad_step,
    field,
    decay,
    spread_left,
    spread_right,
    corr,
    slab,
    group,
    local_scale,
    local_part,
    group_send,
    group_recv,
    group_scale,
    back,
    seeds,
    total_send,
    part,
    from_x,
    z_out,
    from_z,
    send1,
    recv1,
    send2,
    recv2,
    send3,
    recv3,
    send4,
    recv4,
    send5,
    recv5,
    send6,
    recv6,
    send7,
    recv7,
    send8,
):
    nx, nz, ny, nc = sizes
    views, depth, width = weight.shape
    blocks = width // LANES
    wide = views * width // nc
    per_view = width // wide
    depth_total = depth * ny * nc
    vi, di = lax.axis_index("views"), lax.axis_index("depth")
    x, zh = vi // nz, vi % nz
    y, c = di // nc, di % nc

    def in_group(k):
        return y * nc + k

    def in_y(k):
        return k * nc + c

    def in_x(k):
        return k * nz + zh

    def in_z(k):
        return x * nz + k

    own_view, own_base = c // per_view, pl.multiple_of((c % per_view) * wide, LANES)
    own_at = pl.ds(own_base, wide)
    middle = width // 2
    fetches = [
        pltpu.make_async_copy(src, dst, fetched.at[i])
        for i, (src, dst) in enumerate(
            [
                (conc_in, conc),
                (weight_in, weight),
                (index_in.at[:, :, middle : middle + LANES], shifts),
                (att_in, att),
                (yields_in, yields),
                (line_in, line),
            ]
            + [(measured_in.at[own_view, e, :, own_at], measured.at[e]) for e in range(TILE)]
        )
    ]
    for fetch in fetches:
        fetch.start()

    def start_of(v, d):
        return jnp.clip(shifts[v, d, 0] - (middle - LANES), 0, 2 * LANES)

    barrier = pltpu.get_barrier_semaphore()
    greeted = 0
    for k in range(1, nc):
        pl.semaphore_signal(barrier, inc=1, device_id={"depth": in_group((c + k) % nc)}, device_id_type=MESH)
        greeted += 1
    for k in range(1, ny):
        pl.semaphore_signal(barrier, inc=1, device_id={"depth": in_y((y + k) % ny)}, device_id_type=MESH)
        greeted += 1
    for k in range(1, nx):
        pl.semaphore_signal(barrier, inc=1, device_id={"views": in_x((x + k) % nx)}, device_id_type=MESH)
        greeted += 1
    for k in range(1, nz):
        pl.semaphore_signal(barrier, inc=1, device_id={"views": in_z((zh + k) % nz)}, device_id_type=MESH)
        greeted += 1

    for fetch in fetches[3:6]:
        fetch.wait()

    rows16 = lax.broadcasted_iota(jnp.int32, (2 * TILE, depth * TILE), 0)
    cols16 = lax.broadcasted_iota(jnp.int32, (2 * TILE, depth * TILE), 1)
    row_item, col_item, col_depth = rows16 & (TILE - 1), cols16 & (TILE - 1), cols16 // TILE

    def spread(item, values):
        result = jnp.full(item.shape, values[0])
        for i in range(1, TILE):
            result = jnp.where(item == i, values[i], result)
        return result

    att_col = [spread(col_item, [att[k, e] for e in range(TILE)]) for k in range(4)]
    att_row = [spread(row_item, [att[k, e] for e in range(TILE)]) for k in range(4)]
    line_col = spread(col_item, [line[e] for e in range(TILE)])
    line_row = spread(row_item, [line[e] for e in range(TILE)])

    def pick(which, options):
        return jnp.where(which == 0, options[0], jnp.where(which == 1, options[1], options[2]))

    forward_out = pick(line_row, att_col[1:])
    adjoint_out = pick(line_col, att_row[1:])
    for i in range(depth // 2):
        here = rows16 // TILE + 2 * i
        rows = pl.ds(2 * TILE * i, 2 * TILE)
        mat = jnp.where(col_depth < here, att_col[0], jnp.where(col_depth > here, forward_out, 0.0))
        mat_high[rows, :], mat_low[rows, :] = split(mat)
        adj = jnp.where(col_depth > here, att_row[0], jnp.where(col_depth < here, adjoint_out, 0.0))
        adj_high[rows, :], adj_low[rows, :] = split(adj)
    att_tile = [value[:TILE, :LANES] for value in att_row]
    line_tile = line_row[:TILE, :LANES]
    yield_tile = spread(row_item[:TILE, :LANES], [yields[e] for e in range(TILE)])

    def over(tile, columns):
        return jnp.concatenate([tile] * (columns // LANES), axis=1)

    lane = lax.broadcasted_iota(jnp.int32, (TILE, LANES), 1)
    sub = lax.broadcasted_iota(jnp.int32, (TILE, LANES), 0)

    fetches[0].wait()

    def turn_rows(i, carry):
        at = pl.ds(pl.multiple_of(i * TILE, TILE), TILE)
        for j in range(blocks):
            columns = slice(j * LANES, (j + 1) * LANES)
            part[at, :, columns] = jnp.transpose(conc[:, at, columns], (1, 0, 2))
        return carry

    lax.fori_loop(0, depth // TILE, turn_rows, 0)

    def pad_row(d, carry):
        x_blocks = [part[d, :, j * LANES : (j + 1) * LANES] for j in range(blocks)]
        turned = [pltpu.roll(block, LANES - 1, 1) for block in x_blocks]

        def lane_of(block, at):
            return jnp.broadcast_to(block[:, at : at + 1], (TILE, LANES))

        first, second = lane_of(x_blocks[0], 0), lane_of(x_blocks[0], 1)
        before_last, last = lane_of(x_blocks[-1], LANES - 2), lane_of(x_blocks[-1], LANES - 1)
        pad_left[d, 0] = first
        pad_step[d, 0] = second - first
        for j in range(blocks):
            if j < blocks - 1:
                left = x_blocks[j]
                right = jnp.where(lane == LANES - 1, turned[j + 1], turned[j])
            else:
                left = jnp.where(lane == LANES - 1, before_last, x_blocks[j])
                right = jnp.where(lane == LANES - 1, last, turned[j])
            pad_left[d, j + 1] = left
            pad_step[d, j + 1] = right - left
        for j in (blocks + 1, blocks + 2):
            pad_left[d, j] = before_last
            pad_step[d, j] = last - before_last
        return carry

    lax.fori_loop(0, depth, pad_row, 0, unroll=4)

    for fetch in fetches[1:3]:
        fetch.wait()

    for v in range(views):

        def take_row(d, row, shares, sums):
            start = start_of(v, d)
            block, rest = start >> 7, start & (LANES - 1)
            turn = (LANES - rest) & (LANES - 1)
            left = pltpu.roll(pad_left[d, pl.ds(block, blocks + 1)], turn, 2)
            step = pltpu.roll(pad_step[d, pl.ds(block, blocks + 1)], turn, 2)
            whole = lane < LANES - rest
            new = []
            for j in range(blocks):
                at = pl.ds(j * LANES, LANES)
                share = jnp.broadcast_to(shares[row : row + 1, j * LANES : (j + 1) * LANES], (TILE, LANES))
                value = jnp.where(whole, left[j], left[j + 1]) + share * jnp.where(whole, step[j], step[j + 1])
                field[v, pl.ds(pl.multiple_of(d * TILE, TILE), TILE), at] = value
                new.append(sums[j] + value)
            return tuple(new)

        def take_rows(i, sums):
            base = pl.multiple_of(i * TILE, TILE)
            shares = weight[v, pl.ds(base, TILE), :]
            for row in range(TILE):
                sums = take_row(base + row, row, shares, sums)
            return sums

        zero = jnp.zeros((TILE, LANES), F32)
        sums = lax.fori_loop(0, depth // TILE, take_rows, (zero,) * blocks)
        for j in range(blocks):
            chunk, offset = divmod((v * width + j * LANES), wide)
            absorbed = jnp.zeros((TILE, LANES), F32)
            for k in range(4):
                level = jnp.sum(att_tile[k] * sums[j], axis=0, keepdims=True)
                absorbed = jnp.where(sub == k, jnp.broadcast_to(level, (TILE, LANES)), absorbed)
            slab[chunk, TILE:, offset : offset + LANES] = absorbed

    pl.semaphore_wait(barrier, greeted)

    def to_group(k):
        return pltpu.make_async_remote_copy(
            src_ref=slab.at[k],
            dst_ref=group.at[c],
            send_sem=send1.at[k],
            recv_sem=recv1.at[c],
            device_id={"depth": in_group(k)},
            device_id_type=MESH,
        )

    def emit_chunk(chunk):
        v, base = chunk // per_view, (chunk % per_view) * wide
        for part_at in range(0, wide, STEP):
            at = pl.ds(pl.multiple_of(base + part_at, STEP), STEP)
            values = field[v, :, at]
            value = jnp.exp(-dot3(mat_high, mat_low, values))
            decay[v, :, at] = value
            value = (value * values).reshape(depth, TILE, STEP)
            slab[chunk, :TILE, part_at : part_at + STEP] = jnp.sum(value, axis=0) * over(yield_tile, STEP)

    def emit(i, carry):
        chunks = [(c + 1 + PAIR * i + k) % nc for k in range(PAIR)]
        for chunk in chunks:
            emit_chunk(chunk)
        for chunk in chunks:

            @pl.when(chunk != c)
            def _():
                to_group(chunk).start()

        return carry

    lax.fori_loop(0, nc // PAIR, emit, 0)
    group[c] = slab[c]

    def from_group(k):
        return pltpu.make_async_remote_copy(
            src_ref=slab.at[k],
            dst_ref=group.at[k],
            send_sem=send1.at[k],
            recv_sem=recv1.at[k],
            device_id={"depth": in_group(k)},
            device_id_type=MESH,
        )

    for k in range(1, nc):
        from_group((c + k) % nc).wait_recv()

    line_wide = over(line_tile, wide)
    att_wide = [over(tile, wide) for tile in att_tile]

    def scales(ref, count):
        first, later = [], []
        for j in range(count):
            levels = [jnp.broadcast_to(ref[j, TILE + k : TILE + k + 1, :], (TILE, wide)) for k in range(4)]
            first.append(levels[0])
            later.append(pick(line_wide, levels[1:]))
        after = [None] * count
        run = jnp.zeros((TILE, wide), F32)
        for j in reversed(range(count)):
            after[j] = run
            run = run + later[j]
        result = []
        run = jnp.zeros((TILE, wide), F32)
        for j in range(count):
            result.append(jnp.exp(-(run + after[j])))
            run = run + first[j]
        return result

    emitted_sum = jnp.zeros((TILE, wide), F32)
    absorbed_sum = jnp.zeros((TILE, wide), F32)
    for j, scale in enumerate(scales(group, nc)):
        piece = group[j, :TILE, :] * scale
        local_scale[j] = scale
        local_part[j] = piece
        emitted_sum += piece
        absorbed_sum += group[j, TILE:, :]
    group_send[:TILE, :] = emitted_sum
    group_send[TILE:, :] = absorbed_sum

    def y_copy(peer, slot):
        return pltpu.make_async_remote_copy(
            src_ref=group_send,
            dst_ref=group_recv.at[slot],
            send_sem=send2.at[peer],
            recv_sem=recv2.at[slot],
            device_id={"depth": in_y(peer)},
            device_id_type=MESH,
        )

    for k in range(1, ny):
        y_copy((y + k) % ny, y).start()
    group_recv[y] = group_send[...]
    for k in range(1, ny):
        y_copy((y + k) % ny, (y + k) % ny).wait_recv()

    total = jnp.zeros((TILE, wide), F32)
    prior = jnp.zeros((TILE, wide), F32)
    following = jnp.zeros((TILE, wide), F32)
    for j, scale in enumerate(scales(group_recv, ny)):
        piece = group_recv[j, :TILE, :] * scale
        group_scale[j] = scale
        total += piece
        prior += jnp.where(j < y, piece, 0.0)
        following += jnp.where(j > y, piece, 0.0)
    for fetch in fetches[6:]:
        fetch.wait()
    counts = total * (1.0 / depth_total)
    misfit = counts - jnp.concatenate([measured[e] for e in range(TILE)], axis=0)
    here_scale = group_scale[y]
    run = following
    for j in reversed(range(nc)):
        level = jnp.sum(misfit * run, axis=0, keepdims=True)
        back[j, TILE:, :] = att_wide[0] * level
        run = run + local_part[j] * here_scale
    run = prior
    yield_wide = over(yield_tile, wide)
    for j in range(nc):
        back[j, :TILE, :] = misfit * yield_wide * local_scale[j] * here_scale
        mixed = misfit * run
        extra = jnp.zeros((TILE, wide), F32)
        for k in range(3):
            level = jnp.sum(jnp.where(line_wide == k, mixed, 0.0), axis=0, keepdims=True)
            extra += att_wide[k + 1] * level
        back[j, TILE:, :] += extra
        run = run + local_part[j] * here_scale

    def seed_copy(peer, slot):
        return pltpu.make_async_remote_copy(
            src_ref=back.at[peer],
            dst_ref=seeds.at[slot],
            send_sem=send3.at[peer],
            recv_sem=recv3.at[slot],
            device_id={"depth": in_group(peer)},
            device_id_type=MESH,
        )

    def total_copy(peer, slot):
        at = pl.ds(pl.multiple_of((slot % per_view) * wide, LANES), wide)
        return pltpu.make_async_remote_copy(
            src_ref=total_send,
            dst_ref=signal.at[slot // per_view, :, at],
            send_sem=send4.at[peer],
            recv_sem=recv4.at[slot],
            device_id={"depth": in_group(peer)},
            device_id_type=MESH,
        )

    for k in range(1, nc):
        seed_copy((c + k) % nc, c).start()
    seeds[c] = back[c]
    total_send[...] = counts
    signal[own_view, :, own_at] = counts
    for k in range(1, nc):
        total_copy((c + k) % nc, c).start()

    def clear(d, carry):
        zeros = jnp.zeros((3, TILE, LANES), F32)
        for v in range(views):
            spread_left[v, d, 0:3] = zeros
            spread_right[v, d, 0:3] = zeros
            spread_left[v, d, 3 + blocks : 5 + blocks] = zeros[:2]
            spread_right[v, d, 3 + blocks : 5 + blocks] = zeros[:2]
        return carry

    lax.fori_loop(0, depth, clear, 0)

    for k in range(1, nc):
        seed_copy((c + k) % nc, (c + k) % nc).wait_recv()

    def adjoint_chunk(chunk, corr):
        v, base = chunk // per_view, (chunk % per_view) * wide
        for part_at in range(0, wide, STEP):
            start = pl.multiple_of(base + part_at, STEP)
            at = pl.ds(start, STEP)
            factor = seeds[chunk, :TILE, part_at : part_at + STEP]
            constant = seeds[chunk, TILE:, part_at : part_at + STEP]
            direct = decay[v, :, at].reshape(depth, TILE, STEP) * factor[None]
            mixed = direct.reshape(depth * TILE, STEP) * field[v, :, at]
            corr[...] = dot3(adj_high, adj_low, mixed)
            for d in range(depth):
                if d % TILE == 0:
                    shares = weight[v, d : d + TILE, at]
                rows = slice(d * TILE, (d + 1) * TILE)
                value = decay[v, rows, at] * factor - corr[rows, :] - constant
                right = value * jnp.broadcast_to(shares[d % TILE : d % TILE + 1], (TILE, STEP))
                left = value - right
                rest = start_of(v, d) & (LANES - 1)
                for j in range(STEP // LANES):
                    to = 3 + start // LANES + j
                    spread_left[v, d, to] = pltpu.roll(left[:, j * LANES : (j + 1) * LANES], rest, 1)
                    spread_right[v, d, to] = pltpu.roll(right[:, j * LANES : (j + 1) * LANES], rest, 1)

    def adjoint(i, carry):
        for k in range(PAIR):
            adjoint_chunk(PAIR * i + k, corr.at[k])
        return carry

    lax.fori_loop(0, nc // PAIR, adjoint, 0)

    share_x = depth // nx
    share_z = share_x // nz

    def x_copy(peer, pz, slot):
        return pltpu.make_async_remote_copy(
            src_ref=part.at[pl.ds(peer * share_x + pz * share_z, share_z)],
            dst_ref=from_x.at[slot, pz],
            send_sem=send5.at[peer, pz],
            recv_sem=recv5.at[slot, pz],
            device_id={"views": in_x(peer)},
            device_id_type=MESH,
        )

    def place(i, carry):
        peer, pz = (x + 1 + i % nx) % nx, (zh + 1 + i // nx) % nz
        first_row = peer * share_x + pz * share_z

        for r in range(share_z):
            d = first_row + r
            lefts = [None] * (blocks + 2)
            rights = [None] * (blocks + 2)
            for v in range(views):
                start = start_of(v, d)
                block, rest = start >> 7, start & (LANES - 1)
                for ref, sums in ((spread_left, lefts), (spread_right, rights)):
                    turned = ref[v, d, pl.ds(2 - block, blocks + 3)]
                    for j in range(blocks + 2):
                        value = jnp.where(lane >= rest, turned[j + 1], turned[j])
                        sums[j] = value if v == 0 else sums[j] + value

            def total_of(value):
                return jnp.sum(value, axis=1, keepdims=True)

            low_left, low_right = total_of(lefts[0]), total_of(rights[0])
            top = lane == LANES - 1
            high_left = total_of(lefts[-1] + jnp.where(top, lefts[-2], 0.0))
            high_right = total_of(rights[-1])
            shifted = [pltpu.roll(rights[j + 1], 1, 1) for j in range(blocks)]
            for j in range(blocks):
                left = lefts[j + 1]
                if j == 0:
                    right = jnp.where(lane == 0, 0.0, shifted[0])
                    left = left + jnp.where(lane == 0, low_left, 0.0) + jnp.where(lane == 1, low_right, 0.0)
                else:
                    right = jnp.where(lane == 0, shifted[j - 1], shifted[j])
                if j == blocks - 1:
                    left = jnp.where(top, high_right + rights[-2], left)
                    left = left + jnp.where(lane == LANES - 2, high_left, 0.0)
                part[d, :, j * LANES : (j + 1) * LANES] = left + right

        @pl.when(peer != x)
        def _():
            x_copy(peer, pz, x).start()

        return carry

    lax.fori_loop(0, nx * nz, place, 0)

    def arrived(pz):
        for k in range(1, nx):
            x_copy((x + k) % nx, pz, (x + k) % nx).wait_recv()

    def reduced(pz, r):
        value = part[x * share_x + pz * share_z + r]
        for k in range(1, nx):
            value = value + from_x[(x + k) % nx, pz, r]
        return value

    def z_copy(peer, slot):
        return pltpu.make_async_remote_copy(
            src_ref=z_out.at[peer],
            dst_ref=from_z.at[slot],
            send_sem=send6.at[peer],
            recv_sem=recv6.at[slot],
            device_id={"views": in_z(peer)},
            device_id_type=MESH,
        )

    for k in range(1, nz):
        peer = (zh + k) % nz
        arrived(peer)

        def gather_z(r, carry):
            z_out[peer, r] = reduced(peer, r)
            return carry

        lax.fori_loop(0, share_z, gather_z, 0)
        z_copy(peer, zh).start()

    arrived(zh)

    def own(r, carry):
        z_out[zh, r] = reduced(zh, r)
        return carry

    lax.fori_loop(0, share_z, own, 0)
    for k in range(1, nz):
        z_copy((zh + k) % nz, (zh + k) % nz).wait_recv()

    def finish(r, carry):
        value = z_out[zh, r]
        for k in range(1, nz):
            value = value + from_z[(zh + k) % nz, r]
        grad[x * share_x + zh * share_z + r] = value
        return carry

    lax.fori_loop(0, share_z, finish, 0)

    def piece(px, pz):
        return grad.at[pl.ds(px * share_x + pz * share_z, share_z)]

    def give_x(peer, px, pz):
        return pltpu.make_async_remote_copy(
            src_ref=piece(px, pz),
            dst_ref=piece(px, pz),
            send_sem=send7.at[peer, pz],
            recv_sem=recv7.at[px, pz],
            device_id={"views": in_x(peer)},
            device_id_type=MESH,
        )

    def give_z(peer, px, pz):
        return pltpu.make_async_remote_copy(
            src_ref=piece(px, pz),
            dst_ref=piece(px, pz),
            send_sem=send8.at[peer],
            recv_sem=recv7.at[px, pz],
            device_id={"views": in_z(peer)},
            device_id_type=MESH,
        )

    for k in range(1, nz):
        give_z((zh + k) % nz, x, zh).start()
    for k in range(1, nx):
        give_x((x + k) % nx, x, zh).start()
    for k in range(1, nz):
        pz = (zh + k) % nz
        give_z(pz, x, pz).wait_recv()
        for m in range(1, nx):
            give_x((x + m) % nx, x, pz).start()
    for k in range(nz):
        pz = (zh + k) % nz
        for m in range(1, nx):
            give_x((x + m) % nx, (x + m) % nx, pz).wait_recv()
    for k in range(1, nc):
        total_copy((c + k) % nc, (c + k) % nc).wait_recv()

    for k in range(1, nc):
        peer = (c + k) % nc
        to_group(peer).wait_send()
        seed_copy(peer, c).wait_send()
        total_copy(peer, c).wait_send()
    for k in range(1, ny):
        y_copy((y + k) % ny, y).wait_send()
    for k in range(1, nx):
        peer = (x + k) % nx
        for pz in range(nz):
            x_copy(peer, pz, x).wait_send()
            give_x(peer, x, pz).wait_send()
    for k in range(1, nz):
        peer = (zh + k) % nz
        z_copy(peer, zh).wait_send()
        give_z(peer, x, zh).wait_send()


def body(sizes, concentration, shear_index, shear_weight, attenuation, yields, line_energy, measured):
    elements, rows, depth, width = concentration.shape
    views = shear_index.shape[0]
    nx, nz, ny, nc = sizes
    wide = views * width // nc
    blocks = width // LANES
    hbm = pl.BlockSpec(memory_space=pltpu.HBM)
    vmem = pl.BlockSpec(memory_space=pltpu.VMEM)
    full = depth * elements

    def buf(*shape):
        return pltpu.VMEM(shape, F32)

    def sems(*shape):
        return pltpu.SemaphoreType.DMA(shape)

    gradient, signal = pl.pallas_call(
        functools.partial(kernel, sizes),
        out_shape=(
            pltpu.VMEM((depth, elements, width), F32),
            pltpu.VMEM((views, elements, width), F32),
        ),
        in_specs=[hbm] * 7,
        out_specs=(vmem, vmem),
        scratch_shapes=[
            pltpu.SMEM((views, depth, LANES), jnp.int32),
            pltpu.SMEM(attenuation.shape, F32),
            pltpu.SMEM(yields.shape, F32),
            pltpu.SMEM(line_energy.shape, jnp.int32),
            buf(elements, depth, width),
            buf(views, depth, width),
            buf(elements, rows, wide),
            sems(6 + elements),
        ]
        + [pltpu.VMEM((full, full), BF16)] * 4
        + [buf(depth, blocks + 3, elements, LANES)] * 2
        + [buf(views, full, width)] * 2
        + [buf(views, depth, blocks + 5, elements, LANES)] * 2
        + [
            buf(PAIR, full, STEP),
            buf(nc, 2 * elements, wide),
            buf(nc, 2 * elements, wide),
            buf(nc, elements, wide),
            buf(nc, elements, wide),
            buf(2 * elements, wide),
            buf(ny, 2 * elements, wide),
            buf(ny, elements, wide),
            buf(nc, 2 * elements, wide),
            buf(nc, 2 * elements, wide),
            buf(elements, wide),
            buf(depth, elements, width),
            buf(nx, nz, depth // nx // nz, elements, width),
            buf(nz, depth // nx // nz, elements, width),
            buf(nz, depth // nx // nz, elements, width),
        ]
        + [sems(nc)] * 2
        + [sems(ny)] * 2
        + [sems(nc)] * 4
        + [sems(nx, nz)] * 2
        + [sems(nz)] * 2
        + [sems(nx, nz)] * 2
        + [sems(nz)],
        compiler_params=pltpu.CompilerParams(
            collective_id=0, has_side_effects=True, vmem_limit_bytes=56 * 1024 * 1024
        ),
    )(
        shear_index,
        attenuation,
        yields,
        line_energy,
        concentration.reshape(elements, depth, width),
        shear_weight,
        measured,
    )
    gradient = jnp.transpose(gradient, (1, 0, 2)).reshape(elements, rows, depth, width)
    return gradient, signal.reshape(views, elements, rows, width)


SIZES = {(8, 64): (4, 2, 8, 8)}


def solution(mesh):
    sizes = SIZES[mesh.shape["views"], mesh.shape["depth"]]
    return jax.shard_map(
        functools.partial(body, sizes),
        mesh=mesh,
        in_specs=(
            P(None, None, "depth", None),
            P("views", "depth", None),
            P("views", "depth", None),
            P(),
            P(),
            P(),
            P("views", None, None, None),
        ),
        out_specs=(P(None, None, "depth", None), P("views", None, None, None)),
        check_vma=False,
    )
```

```python
import functools

import jax
import jax.numpy as jnp
from jax import lax
from jax.experimental import pallas as pl
from jax.experimental.pallas import tpu as pltpu
from jax.sharding import PartitionSpec as P

LANES = 128
TILE = 8
STEP = 256
PAIR = 2
SPLIT = 4
MESH = pl.DeviceIdType.MESH
F32 = jnp.float32
BF16 = jnp.bfloat16


def split(value):
    high = value.astype(BF16)
    low = (value - high.astype(F32)).astype(BF16)
    return high, low


def dot3(high_ref, low_ref, right):
    right_high, right_low = split(right)
    high = high_ref[...]
    result = jnp.dot(high, right_high, preferred_element_type=F32)
    result += jnp.dot(high, right_low, preferred_element_type=F32)
    return result + jnp.dot(low_ref[...], right_high, preferred_element_type=F32)


def kernel(
    sizes,
    index_in,
    att_in,
    yields_in,
    line_in,
    conc_in,
    weight_in,
    measured_in,
    grad,
    signal,
    shifts,
    att,
    yields,
    line,
    conc,
    weight,
    measured,
    fetched,
    mat_high,
    mat_low,
    adj_high,
    adj_low,
    pad_left,
    pad_step,
    field,
    decay,
    spread_left,
    spread_right,
    corr,
    slab,
    group,
    local_scale,
    local_part,
    group_send,
    group_recv,
    group_scale,
    back,
    seeds,
    total_send,
    part,
    from_x,
    z_out,
    from_z,
    send1,
    recv1,
    send2,
    recv2,
    send3,
    recv3,
    send4,
    recv4,
    send5,
    recv5,
    send6,
    recv6,
    send7,
    recv7,
    send8,
):
    nx, nz, ny, nc = sizes
    views, depth, width = weight.shape
    blocks = width // LANES
    wide = views * width // nc
    per_view = width // wide
    tiles = wide // LANES
    depth_total = depth * ny * nc
    vi, di = lax.axis_index("views"), lax.axis_index("depth")
    x, zh = vi // nz, vi % nz
    y, c = di // nc, di % nc

    def flip(k):
        bits = [((c // b + k // b) % 2) * b for b in (1, 2, 4) if b < nc]
        return sum(bits)

    def in_group(k):
        return y * nc + k

    def in_y(k):
        return k * nc + c

    def in_x(k):
        return k * nz + zh

    def in_z(k):
        return x * nz + k

    own_view, own_base = c // per_view, pl.multiple_of((c % per_view) * wide, LANES)
    own_at = pl.ds(own_base, wide)
    middle = width // 2
    fetches = [
        pltpu.make_async_copy(src, dst, fetched.at[i])
        for i, (src, dst) in enumerate(
            [
                (conc_in, conc),
                (weight_in, weight),
                (index_in.at[:, :, middle : middle + LANES], shifts),
                (att_in, att),
                (yields_in, yields),
                (line_in, line),
            ]
            + [(measured_in.at[own_view, e, :, own_at], measured.at[e]) for e in range(TILE)]
        )
    ]
    for fetch in fetches:
        fetch.start()

    def start_of(v, d):
        return jnp.clip(shifts[v, d, 0] - (middle - LANES), 0, 2 * LANES)

    barrier = pltpu.get_barrier_semaphore()
    greeted = 0
    for k in range(1, nc):
        pl.semaphore_signal(barrier, inc=1, device_id={"depth": in_group((c + k) % nc)}, device_id_type=MESH)
        greeted += 1
    for k in range(1, ny):
        pl.semaphore_signal(barrier, inc=1, device_id={"depth": in_y((y + k) % ny)}, device_id_type=MESH)
        greeted += 1
    for k in range(1, nx):
        pl.semaphore_signal(barrier, inc=1, device_id={"views": in_x((x + k) % nx)}, device_id_type=MESH)
        greeted += 1
    for k in range(1, nz):
        pl.semaphore_signal(barrier, inc=1, device_id={"views": in_z((zh + k) % nz)}, device_id_type=MESH)
        greeted += 1

    for fetch in fetches[3:6]:
        fetch.wait()

    rows16 = lax.broadcasted_iota(jnp.int32, (2 * TILE, depth * TILE), 0)
    cols16 = lax.broadcasted_iota(jnp.int32, (2 * TILE, depth * TILE), 1)
    row_item, col_item, col_depth = rows16 & (TILE - 1), cols16 & (TILE - 1), cols16 // TILE

    def spread(item, values):
        result = jnp.full(item.shape, values[0])
        for i in range(1, TILE):
            result = jnp.where(item == i, values[i], result)
        return result

    att_col = [spread(col_item, [att[k, e] for e in range(TILE)]) for k in range(4)]
    att_row = [spread(row_item, [att[k, e] for e in range(TILE)]) for k in range(4)]
    line_col = spread(col_item, [line[e] for e in range(TILE)])
    line_row = spread(row_item, [line[e] for e in range(TILE)])

    def pick(which, options):
        return jnp.where(which == 0, options[0], jnp.where(which == 1, options[1], options[2]))

    forward_out = pick(line_row, att_col[1:])
    adjoint_out = pick(line_col, att_row[1:])
    for i in range(depth // 2):
        here = rows16 // TILE + 2 * i
        rows = pl.ds(2 * TILE * i, 2 * TILE)
        mat = jnp.where(col_depth < here, att_col[0], jnp.where(col_depth > here, forward_out, 0.0))
        mat_high[rows, :], mat_low[rows, :] = split(mat)
        adj = jnp.where(col_depth > here, att_row[0], jnp.where(col_depth < here, adjoint_out, 0.0))
        adj_high[rows, :], adj_low[rows, :] = split(adj)
    att_tile = [value[:TILE, :LANES] for value in att_row]
    line_tile = line_row[:TILE, :LANES]
    yield_tile = spread(row_item[:TILE, :LANES], [yields[e] for e in range(TILE)])

    def over(tile, columns):
        return jnp.concatenate([tile] * (columns // LANES), axis=1)

    lane = lax.broadcasted_iota(jnp.int32, (TILE, LANES), 1)
    sub = lax.broadcasted_iota(jnp.int32, (TILE, LANES), 0)

    def stack_rows(levels):
        result = jnp.broadcast_to(levels[0], (TILE, LANES))
        for k in range(1, TILE):
            result = jnp.where(sub == k, jnp.broadcast_to(levels[k], (TILE, LANES)), result)
        return result

    def columns_of(ref, j):
        return jnp.concatenate([ref[j, b] for b in range(tiles)], axis=1)

    def packed_row(ref, j, b, k):
        at = 4 * (b % 2) + k
        return jnp.broadcast_to(ref[j, tiles + b // 2, at : at + 1, :], (TILE, LANES))

    fetches[0].wait()

    def turn_rows(i, carry):
        at = pl.ds(pl.multiple_of(i * TILE, TILE), TILE)
        for j in range(blocks):
            columns = slice(j * LANES, (j + 1) * LANES)
            part[at, :, columns] = jnp.transpose(conc[:, at, columns], (1, 0, 2))
        return carry

    lax.fori_loop(0, depth // TILE, turn_rows, 0)

    def pad_row(d, carry):
        x_blocks = [part[d, :, j * LANES : (j + 1) * LANES] for j in range(blocks)]
        turned = [pltpu.roll(block, LANES - 1, 1) for block in x_blocks]

        def lane_of(block, at):
            return jnp.broadcast_to(block[:, at : at + 1], (TILE, LANES))

        first, second = lane_of(x_blocks[0], 0), lane_of(x_blocks[0], 1)
        before_last, last = lane_of(x_blocks[-1], LANES - 2), lane_of(x_blocks[-1], LANES - 1)
        pad_left[d, 0] = first
        pad_step[d, 0] = second - first
        for j in range(blocks):
            if j < blocks - 1:
                left = x_blocks[j]
                right = jnp.where(lane == LANES - 1, turned[j + 1], turned[j])
            else:
                left = jnp.where(lane == LANES - 1, before_last, x_blocks[j])
                right = jnp.where(lane == LANES - 1, last, turned[j])
            pad_left[d, j + 1] = left
            pad_step[d, j + 1] = right - left
        for j in (blocks + 1, blocks + 2):
            pad_left[d, j] = before_last
            pad_step[d, j] = last - before_last
        return carry

    lax.fori_loop(0, depth, pad_row, 0, unroll=4)

    for fetch in fetches[1:3]:
        fetch.wait()

    for v in range(views):

        def take_row(d, row, shares, sums):
            start = start_of(v, d)
            block, rest = start >> 7, start & (LANES - 1)
            turn = (LANES - rest) & (LANES - 1)
            left = pltpu.roll(pad_left[d, pl.ds(block, blocks + 1)], turn, 2)
            step = pltpu.roll(pad_step[d, pl.ds(block, blocks + 1)], turn, 2)
            whole = lane < LANES - rest
            new = []
            for j in range(blocks):
                at = pl.ds(j * LANES, LANES)
                share = jnp.broadcast_to(shares[row : row + 1, j * LANES : (j + 1) * LANES], (TILE, LANES))
                value = jnp.where(whole, left[j], left[j + 1]) + share * jnp.where(whole, step[j], step[j + 1])
                field[v, pl.ds(pl.multiple_of(d * TILE, TILE), TILE), at] = value
                new.append(sums[j] + value)
            return tuple(new)

        def take_rows(i, sums):
            base = pl.multiple_of(i * TILE, TILE)
            shares = weight[v, pl.ds(base, TILE), :]
            for row in range(TILE):
                sums = take_row(base + row, row, shares, sums)
            return sums

        zero = jnp.zeros((TILE, LANES), F32)
        sums = lax.fori_loop(0, depth // TILE, take_rows, (zero,) * blocks)
        for j in range(0, blocks, 2):
            chunk, offset = divmod(v * blocks + j, tiles)
            levels = [
                jnp.sum(att_tile[k] * sums[j + h], axis=0, keepdims=True) for h in range(2) for k in range(4)
            ]
            slab[chunk, tiles + offset // 2] = stack_rows(levels)

    pl.semaphore_wait(barrier, greeted)

    def to_group(k):
        return pltpu.make_async_remote_copy(
            src_ref=slab.at[k],
            dst_ref=group.at[c],
            send_sem=send1.at[k],
            recv_sem=recv1.at[c],
            device_id={"depth": in_group(k)},
            device_id_type=MESH,
        )

    def emit_chunk(chunk):
        v, base = chunk // per_view, (chunk % per_view) * wide
        for part_at in range(0, wide, STEP):
            at = pl.ds(pl.multiple_of(base + part_at, STEP), STEP)
            values = field[v, :, at]
            value = jnp.exp(-dot3(mat_high, mat_low, values))
            decay[v, :, at] = value
            value = (value * values).reshape(depth, TILE, STEP)
            value = jnp.sum(value, axis=0)
            for j in range(STEP // LANES):
                slab[chunk, part_at // LANES + j] = value[:, j * LANES : (j + 1) * LANES] * yield_tile

    def emit(i, carry):
        chunks = [flip(nc - PAIR * (i + 1) + k) for k in range(PAIR)]
        for chunk in chunks:
            emit_chunk(chunk)
        for chunk in chunks:

            @pl.when(chunk != c)
            def _():
                to_group(chunk).start()

        return carry

    lax.fori_loop(0, nc // PAIR, emit, 0)
    group[c] = slab[c]

    def from_group(k):
        return pltpu.make_async_remote_copy(
            src_ref=slab.at[k],
            dst_ref=group.at[k],
            send_sem=send1.at[k],
            recv_sem=recv1.at[k],
            device_id={"depth": in_group(k)},
            device_id_type=MESH,
        )

    for k in range(1, nc):
        from_group((c + k) % nc).wait_recv()

    line_wide = over(line_tile, wide)

    def scales(ref, count):
        first, later = [], []
        for j in range(count):
            levels = [
                jnp.concatenate([packed_row(ref, j, b, k) for b in range(tiles)], axis=1) for k in range(4)
            ]
            first.append(levels[0])
            later.append(pick(line_wide, levels[1:]))
        after = [None] * count
        run = jnp.zeros((TILE, wide), F32)
        for j in reversed(range(count)):
            after[j] = run
            run = run + later[j]
        result = []
        run = jnp.zeros((TILE, wide), F32)
        for j in range(count):
            result.append(jnp.exp(-(run + after[j])))
            run = run + first[j]
        return result

    emitted_sum = jnp.zeros((TILE, wide), F32)
    for j, scale in enumerate(scales(group, nc)):
        piece = columns_of(group, j) * scale
        local_scale[j] = scale
        local_part[j] = piece
        emitted_sum += piece
    for b in range(tiles):
        group_send[b] = emitted_sum[:, b * LANES : (b + 1) * LANES]
    for b in range(tiles, tiles + tiles // 2):
        value = group[0, b]
        for j in range(1, nc):
            value = value + group[j, b]
        group_send[b] = value

    def y_copy(peer, slot):
        return pltpu.make_async_remote_copy(
            src_ref=group_send,
            dst_ref=group_recv.at[slot],
            send_sem=send2.at[peer],
            recv_sem=recv2.at[slot],
            device_id={"depth": in_y(peer)},
            device_id_type=MESH,
        )

    for k in sorted(range(1, ny), key=lambda k: -min(k, ny - k)):
        y_copy((y + k) % ny, y).start()
    group_recv[y] = group_send[...]
    for k in range(1, ny):
        y_copy((y + k) % ny, (y + k) % ny).wait_recv()

    total = jnp.zeros((TILE, wide), F32)
    prior = jnp.zeros((TILE, wide), F32)
    following = jnp.zeros((TILE, wide), F32)
    for j, scale in enumerate(scales(group_recv, ny)):
        piece = columns_of(group_recv, j) * scale
        group_scale[j] = scale
        total += piece
        prior += jnp.where(j < y, piece, 0.0)
        following += jnp.where(j > y, piece, 0.0)
    for fetch in fetches[6:]:
        fetch.wait()
    counts = total * (1.0 / depth_total)
    misfit = counts - jnp.concatenate([measured[e] for e in range(TILE)], axis=0)
    here_scale = group_scale[y]
    later = [None] * nc
    run = following
    for j in reversed(range(nc)):
        later[j] = jnp.sum(misfit * run, axis=0, keepdims=True)
        run = run + local_part[j] * here_scale
    run = prior
    yield_wide = over(yield_tile, wide)
    for j in range(nc):
        value = misfit * yield_wide * local_scale[j] * here_scale
        for b in range(tiles):
            back[j, b] = value[:, b * LANES : (b + 1) * LANES]
        mixed = misfit * run
        levels = [later[j]] + [
            jnp.sum(jnp.where(line_wide == k, mixed, 0.0), axis=0, keepdims=True) for k in range(3)
        ]
        for b in range(0, tiles, 2):
            back[j, tiles + b // 2] = stack_rows(
                [level[:, (b + h) * LANES : (b + h + 1) * LANES] for h in range(2) for level in levels]
            )
        run = run + local_part[j] * here_scale

    def seed_copy(peer, slot):
        return pltpu.make_async_remote_copy(
            src_ref=back.at[peer],
            dst_ref=seeds.at[slot],
            send_sem=send3.at[peer],
            recv_sem=recv3.at[slot],
            device_id={"depth": in_group(peer)},
            device_id_type=MESH,
        )

    def total_copy(peer, slot):
        at = pl.ds(pl.multiple_of((slot % per_view) * wide, LANES), wide)
        return pltpu.make_async_remote_copy(
            src_ref=total_send,
            dst_ref=signal.at[slot // per_view, :, :, at],
            send_sem=send4.at[peer],
            recv_sem=recv4.at[slot],
            device_id={"depth": in_group(peer)},
            device_id_type=MESH,
        )

    for k in reversed(range(1, nc)):
        seed_copy(flip(k), c).start()
    seeds[c] = back[c]
    for e in range(TILE):
        total_send[e] = counts[e : e + 1]
        signal[own_view, e, :, own_at] = counts[e : e + 1]
    for k in range(1, nc):
        total_copy((c + k) % nc, c).start()

    def clear(d, carry):
        zeros = jnp.zeros((3, TILE, LANES), F32)
        for v in range(views):
            spread_left[v, d, 0:3] = zeros
            spread_right[v, d, 0:3] = zeros
            spread_left[v, d, 3 + blocks : 5 + blocks] = zeros[:2]
            spread_right[v, d, 3 + blocks : 5 + blocks] = zeros[:2]
        return carry

    lax.fori_loop(0, depth, clear, 0)

    def adjoint_chunk(chunk, corr):
        v, base = chunk // per_view, (chunk % per_view) * wide
        for part_at in range(0, wide, STEP):
            start = pl.multiple_of(base + part_at, STEP)
            at = pl.ds(start, STEP)
            here = range(part_at // LANES, (part_at + STEP) // LANES)
            factor = jnp.concatenate([seeds[chunk, b] for b in here], axis=1)
            constant = jnp.concatenate(
                [sum(att_tile[k] * packed_row(seeds, chunk, b, k) for k in range(4)) for b in here], axis=1
            )
            direct = decay[v, :, at].reshape(depth, TILE, STEP) * factor[None]
            mixed = direct.reshape(depth * TILE, STEP) * field[v, :, at]
            corr[...] = dot3(adj_high, adj_low, mixed)
            for d in range(depth):
                if d % TILE == 0:
                    shares = weight[v, d : d + TILE, at]
                rows = slice(d * TILE, (d + 1) * TILE)
                value = decay[v, rows, at] * factor - corr[rows, :] - constant
                right = value * jnp.broadcast_to(shares[d % TILE : d % TILE + 1], (TILE, STEP))
                left = value - right
                rest = start_of(v, d) & (LANES - 1)
                for j in range(STEP // LANES):
                    to = 3 + start // LANES + j
                    spread_left[v, d, to] = pltpu.roll(left[:, j * LANES : (j + 1) * LANES], rest, 1)
                    spread_right[v, d, to] = pltpu.roll(right[:, j * LANES : (j + 1) * LANES], rest, 1)

    def adjoint(i, carry):
        chunks = [flip(PAIR * i + k) for k in range(PAIR)]
        for chunk in chunks:

            @pl.when(chunk != c)
            def _():
                seed_copy(chunk, chunk).wait_recv()

        for k, chunk in enumerate(chunks):
            adjoint_chunk(chunk, corr.at[k])
        return carry

    lax.fori_loop(0, nc // PAIR, adjoint, 0)

    share_x = depth // nx
    share_z = share_x // nz
    share = share_z // SPLIT

    def row_of(px, pz, s):
        return px * share_x + pz * share_z + s * share

    def x_copy(peer, pz, s, slot):
        return pltpu.make_async_remote_copy(
            src_ref=part.at[pl.ds(row_of(peer, pz, s), share)],
            dst_ref=from_x.at[slot, pz, s],
            send_sem=send5.at[peer, pz, s],
            recv_sem=recv5.at[slot, pz, s],
            device_id={"views": in_x(peer)},
            device_id_type=MESH,
        )

    def place(i, carry):
        pz, s = (zh + 1 + i // SPLIT) % nz, i % SPLIT
        for d in [row_of((x + 1 + k) % nx, pz, s) + r for k in range(nx) for r in range(share)]:
            lefts = [None] * (blocks + 2)
            rights = [None] * (blocks + 2)
            for v in range(views):
                start = start_of(v, d)
                block, rest = start >> 7, start & (LANES - 1)
                for ref, sums in ((spread_left, lefts), (spread_right, rights)):
                    turned = ref[v, d, pl.ds(2 - block, blocks + 3)]
                    for j in range(blocks + 2):
                        value = jnp.where(lane >= rest, turned[j + 1], turned[j])
                        sums[j] = value if v == 0 else sums[j] + value

            def total_of(value):
                return jnp.sum(value, axis=1, keepdims=True)

            low_left, low_right = total_of(lefts[0]), total_of(rights[0])
            top = lane == LANES - 1
            high_left = total_of(lefts[-1] + jnp.where(top, lefts[-2], 0.0))
            high_right = total_of(rights[-1])
            shifted = [pltpu.roll(rights[j + 1], 1, 1) for j in range(blocks)]
            for j in range(blocks):
                left = lefts[j + 1]
                if j == 0:
                    right = jnp.where(lane == 0, 0.0, shifted[0])
                    left = left + jnp.where(lane == 0, low_left, 0.0) + jnp.where(lane == 1, low_right, 0.0)
                else:
                    right = jnp.where(lane == 0, shifted[j - 1], shifted[j])
                if j == blocks - 1:
                    left = jnp.where(top, high_right + rights[-2], left)
                    left = left + jnp.where(lane == LANES - 2, high_left, 0.0)
                part[d, :, j * LANES : (j + 1) * LANES] = left + right

        for k in range(1, nx):
            x_copy((x + k) % nx, pz, s, x).start()
        return carry

    lax.fori_loop(0, nz * SPLIT, place, 0)

    def reduce_x(pz, s):
        for k in range(1, nx):
            x_copy((x + k) % nx, pz, s, (x + k) % nx).wait_recv()
        for r in range(share):
            value = part[row_of(x, pz, s) + r]
            for k in range(1, nx):
                value = value + from_x[(x + k) % nx, pz, s, r]
            z_out[pz, s, r] = value

    def z_copy(peer, s, slot):
        return pltpu.make_async_remote_copy(
            src_ref=z_out.at[peer, s],
            dst_ref=from_z.at[slot, s],
            send_sem=send6.at[peer, s],
            recv_sem=recv6.at[slot, s],
            device_id={"views": in_z(peer)},
            device_id_type=MESH,
        )

    def piece(px, pz, s):
        return grad.at[pl.ds(row_of(px, pz, s), share)]

    def give_x(step, px, pz, s, sem):
        return pltpu.make_async_remote_copy(
            src_ref=piece(px, pz, s),
            dst_ref=piece(px, pz, s),
            send_sem=send7.at[sem, pz, s],
            recv_sem=recv7.at[px, pz, s],
            device_id={"views": in_x((x + step) % nx)},
            device_id_type=MESH,
        )

    def give_z(peer, px, pz, s):
        return pltpu.make_async_remote_copy(
            src_ref=piece(px, pz, s),
            dst_ref=piece(px, pz, s),
            send_sem=send8.at[peer, s],
            recv_sem=recv7.at[px, pz, s],
            device_id={"views": in_z(peer)},
            device_id_type=MESH,
        )

    for s in range(SPLIT):
        for k in range(1, nz):
            reduce_x((zh + k) % nz, s)
            z_copy((zh + k) % nz, s, zh).start()

    steps = [1] if nx == 2 else [1, nx - 1]
    sent, waited = [], set()

    def give(copy):
        copy.start()
        sent.append(copy)

    def spread_x(pz, s):
        for sem, step in enumerate(steps):
            give(give_x(step, x, pz, s, sem))

    def receive(step, turn, s):
        px, pz = (x + step) % nx, (zh + turn) % nz
        give_x(0, px, pz, s, 0).wait_recv()
        waited.add((step, turn, s))
        return px, pz

    def relay(turn, s):
        if nx == 4:
            onward = 1 if s % 2 == 0 else nx - 1
            px, pz = receive(nx - onward, turn, s)
            give(give_x(onward, px, pz, s, 2))

    for s in range(SPLIT):
        reduce_x(zh, s)
        for k in range(1, nz):
            z_copy((zh + k) % nz, s, (zh + k) % nz).wait_recv()
        for r in range(share):
            value = z_out[zh, s, r]
            for k in range(1, nz):
                value = value + from_z[(zh + k) % nz, s, r]
            grad[row_of(x, zh, s) + r] = value
        for k in range(1, nz):
            give(give_z((zh + k) % nz, x, zh, s))
        spread_x(zh, s)
    for s in range(SPLIT):
        relay(0, s)
        for k in range(1, nz):
            _, pz = receive(0, k, s)
            spread_x(pz, s)
    for k in range(1, nz):
        for s in range(SPLIT):
            relay(k, s)
    for k in range(nz):
        for s in range(SPLIT):
            for step in range(1, nx):
                if (step, k, s) not in waited:
                    receive(step, k, s)
    for k in range(1, nc):
        total_copy((c + k) % nc, (c + k) % nc).wait_recv()

    for k in range(1, nc):
        peer = (c + k) % nc
        to_group(peer).wait_send()
        seed_copy(peer, c).wait_send()
        total_copy(peer, c).wait_send()
    for k in range(1, ny):
        y_copy((y + k) % ny, y).wait_send()
    for k in range(1, nx):
        peer = (x + k) % nx
        for pz in range(nz):
            for s in range(SPLIT):
                x_copy(peer, pz, s, x).wait_send()
    for k in range(1, nz):
        for s in range(SPLIT):
            z_copy((zh + k) % nz, s, zh).wait_send()
    for copy in sent:
        copy.wait_send()


def body(sizes, concentration, shear_index, shear_weight, attenuation, yields, line_energy, measured):
    elements, rows, depth, width = concentration.shape
    views = shear_index.shape[0]
    nx, nz, ny, nc = sizes
    wide = views * width // nc
    tiles = wide // LANES
    blocks = width // LANES
    share = depth // nx // nz // SPLIT
    hbm = pl.BlockSpec(memory_space=pltpu.HBM)
    vmem = pl.BlockSpec(memory_space=pltpu.VMEM)
    full = depth * elements

    def buf(*shape):
        return pltpu.VMEM(shape, F32)

    def sems(*shape):
        return pltpu.SemaphoreType.DMA(shape)

    gradient, signal = pl.pallas_call(
        functools.partial(kernel, sizes),
        out_shape=(
            pltpu.VMEM((depth, elements, width), F32),
            pltpu.VMEM((views, elements, rows, width), F32),
        ),
        in_specs=[hbm] * 7,
        out_specs=(vmem, vmem),
        scratch_shapes=[
            pltpu.SMEM((views, depth, LANES), jnp.int32),
            pltpu.SMEM(attenuation.shape, F32),
            pltpu.SMEM(yields.shape, F32),
            pltpu.SMEM(line_energy.shape, jnp.int32),
            buf(elements, depth, width),
            buf(views, depth, width),
            buf(elements, rows, wide),
            sems(6 + elements),
        ]
        + [pltpu.VMEM((full, full), BF16)] * 4
        + [buf(depth, blocks + 3, elements, LANES)] * 2
        + [buf(views, full, width)] * 2
        + [buf(views, depth, blocks + 5, elements, LANES)] * 2
        + [
            buf(PAIR, full, STEP),
            buf(nc, tiles + tiles // 2, elements, LANES),
            buf(nc, tiles + tiles // 2, elements, LANES),
            buf(nc, elements, wide),
            buf(nc, elements, wide),
            buf(tiles + tiles // 2, elements, LANES),
            buf(ny, tiles + tiles // 2, elements, LANES),
            buf(ny, elements, wide),
            buf(nc, tiles + tiles // 2, elements, LANES),
            buf(nc, tiles + tiles // 2, elements, LANES),
            buf(elements, rows, wide),
            buf(depth, elements, width),
            buf(nx, nz, SPLIT, share, elements, width),
            buf(nz, SPLIT, share, elements, width),
            buf(nz, SPLIT, share, elements, width),
        ]
        + [sems(nc)] * 2
        + [sems(ny)] * 2
        + [sems(nc)] * 4
        + [sems(nx, nz, SPLIT)] * 2
        + [sems(nz, SPLIT)] * 2
        + [sems(3, nz, SPLIT), sems(nx, nz, SPLIT)]
        + [sems(nz, SPLIT)],
        compiler_params=pltpu.CompilerParams(
            collective_id=0, has_side_effects=True, vmem_limit_bytes=56 * 1024 * 1024
        ),
    )(
        shear_index,
        attenuation,
        yields,
        line_energy,
        concentration.reshape(elements, depth, width),
        shear_weight,
        measured,
    )
    gradient = jnp.transpose(gradient, (1, 0, 2)).reshape(elements, rows, depth, width)
    return gradient, signal


SIZES = {(8, 64): (4, 2, 8, 8)}


def solution(mesh):
    sizes = SIZES[mesh.shape["views"], mesh.shape["depth"]]
    return jax.shard_map(
        functools.partial(body, sizes),
        mesh=mesh,
        in_specs=(
            P(None, None, "depth", None),
            P("views", "depth", None),
            P("views", "depth", None),
            P(),
            P(),
            P(),
            P("views", None, None, None),
        ),
        out_specs=(P(None, None, "depth", None), P("views", None, None, None)),
        check_vma=False,
    )
```

```python
import functools

import jax
import jax.numpy as jnp
from jax import lax
from jax.experimental import pallas as pl
from jax.experimental.pallas import tpu as pltpu
from jax.sharding import PartitionSpec as P

LANES = 128
TILE = 8
STEP = 256
PAIR = 2
SPLIT = 4
MESH = pl.DeviceIdType.MESH
F32 = jnp.float32
BF16 = jnp.bfloat16


def split(value):
    high = value.astype(BF16)
    low = (value - high.astype(F32)).astype(BF16)
    return high, low


def dot3(high_ref, low_ref, right):
    right_high, right_low = split(right)
    high = high_ref[...]
    result = jnp.dot(high, right_high, preferred_element_type=F32)
    result += jnp.dot(high, right_low, preferred_element_type=F32)
    return result + jnp.dot(low_ref[...], right_high, preferred_element_type=F32)


def kernel(
    sizes,
    index_in,
    att_in,
    yields_in,
    line_in,
    conc_in,
    weight_in,
    measured_in,
    grad,
    signal,
    shifts,
    att,
    yields,
    line,
    conc,
    weight,
    measured,
    fetched,
    mat_high,
    mat_low,
    adj_high,
    adj_low,
    pad_left,
    pad_step,
    field,
    decay,
    spread_left,
    spread_right,
    corr,
    slab,
    group,
    local_scale,
    local_part,
    group_send,
    group_recv,
    group_scale,
    back,
    seeds,
    total_send,
    part,
    from_x,
    z_out,
    from_z,
    full,
    send1,
    recv1,
    send2,
    recv2,
    send3,
    recv3,
    send4,
    recv4,
    send5,
    recv5,
    send6,
    recv6,
    send7,
    recv7,
    send8,
):
    nx, nz, ny, nc = sizes
    views, depth, width = weight.shape
    blocks = width // LANES
    wide = views * width // nc
    per_view = width // wide
    tiles = wide // LANES
    depth_total = depth * ny * nc
    vi, di = lax.axis_index("views"), lax.axis_index("depth")
    x, zh = vi // nz, vi % nz
    y, c = di // nc, di % nc

    def flip(k):
        bits = [((c // b + k // b) % 2) * b for b in (1, 2, 4) if b < nc]
        return sum(bits)

    def in_group(k):
        return y * nc + k

    def in_y(k):
        return k * nc + c

    def in_x(k):
        return k * nz + zh

    def in_z(k):
        return x * nz + k

    own_view, own_base = c // per_view, pl.multiple_of((c % per_view) * wide, LANES)
    own_at = pl.ds(own_base, wide)
    middle = width // 2
    fetches = [
        pltpu.make_async_copy(src, dst, fetched.at[min(i, 6)])
        for i, (src, dst) in enumerate(
            [
                (conc_in, conc),
                (weight_in, weight),
                (index_in.at[:, :, middle : middle + LANES], shifts),
                (att_in, att),
                (yields_in, yields),
                (line_in, line),
            ]
            + [(measured_in.at[own_view, e, :, own_at], measured.at[e]) for e in range(TILE)]
        )
    ]
    for fetch in fetches:
        fetch.start()

    def start_of(v, d):
        return jnp.clip(shifts[v, d, 0] - (middle - LANES), 0, 2 * LANES)

    def all_of(ref, sem):
        return pltpu.make_async_remote_copy(
            src_ref=ref,
            dst_ref=ref,
            send_sem=sem,
            recv_sem=sem,
            device_id={"depth": in_group(flip(1))},
            device_id_type=MESH,
        )

    barrier = pltpu.get_barrier_semaphore()
    greeted = 0
    for k in range(1, nc):
        pl.semaphore_signal(barrier, inc=1, device_id={"depth": in_group((c + k) % nc)}, device_id_type=MESH)
        greeted += 1
    for k in range(1, ny):
        pl.semaphore_signal(barrier, inc=1, device_id={"depth": in_y((y + k) % ny)}, device_id_type=MESH)
        greeted += 1
    for k in range(1, nx):
        pl.semaphore_signal(barrier, inc=1, device_id={"views": in_x((x + k) % nx)}, device_id_type=MESH)
        greeted += 1
    for k in range(1, nz):
        pl.semaphore_signal(barrier, inc=1, device_id={"views": in_z((zh + k) % nz)}, device_id_type=MESH)
        greeted += 1

    for fetch in fetches[3:6]:
        fetch.wait()

    rows16 = lax.broadcasted_iota(jnp.int32, (2 * TILE, depth * TILE), 0)
    cols16 = lax.broadcasted_iota(jnp.int32, (2 * TILE, depth * TILE), 1)
    row_item, col_item, col_depth = rows16 & (TILE - 1), cols16 & (TILE - 1), cols16 // TILE

    def spread(item, values):
        result = jnp.full(item.shape, values[0])
        for i in range(1, TILE):
            result = jnp.where(item == i, values[i], result)
        return result

    att_col = [spread(col_item, [att[k, e] for e in range(TILE)]) for k in range(4)]
    att_row = [spread(row_item, [att[k, e] for e in range(TILE)]) for k in range(4)]
    line_col = spread(col_item, [line[e] for e in range(TILE)])
    line_row = spread(row_item, [line[e] for e in range(TILE)])

    def pick(which, options):
        return jnp.where(which == 0, options[0], jnp.where(which == 1, options[1], options[2]))

    forward_out = pick(line_row, att_col[1:])
    adjoint_out = pick(line_col, att_row[1:])
    for i in range(depth // 2):
        here = rows16 // TILE + 2 * i
        rows = pl.ds(2 * TILE * i, 2 * TILE)
        mat = jnp.where(col_depth < here, att_col[0], jnp.where(col_depth > here, forward_out, 0.0))
        mat_high[rows, :], mat_low[rows, :] = split(mat)
        adj = jnp.where(col_depth > here, att_row[0], jnp.where(col_depth < here, adjoint_out, 0.0))
        adj_high[rows, :], adj_low[rows, :] = split(adj)
    att_tile = [value[:TILE, :LANES] for value in att_row]
    line_tile = line_row[:TILE, :LANES]
    yield_tile = spread(row_item[:TILE, :LANES], [yields[e] for e in range(TILE)])

    def over(tile, columns):
        return jnp.concatenate([tile] * (columns // LANES), axis=1)

    lane = lax.broadcasted_iota(jnp.int32, (TILE, LANES), 1)
    sub = lax.broadcasted_iota(jnp.int32, (TILE, LANES), 0)

    def stack_rows(levels):
        result = jnp.broadcast_to(levels[0], (TILE, LANES))
        for k in range(1, TILE):
            result = jnp.where(sub == k, jnp.broadcast_to(levels[k], (TILE, LANES)), result)
        return result

    def columns_of(ref, j):
        return jnp.concatenate([ref[j, b] for b in range(tiles)], axis=1)

    def packed_row(ref, j, b, k):
        at = 4 * (b % 2) + k
        return jnp.broadcast_to(ref[j, tiles + b // 2, at : at + 1, :], (TILE, LANES))

    fetches[0].wait()

    def turn_rows(i, carry):
        at = pl.ds(pl.multiple_of(i * TILE, TILE), TILE)
        for j in range(blocks):
            columns = slice(j * LANES, (j + 1) * LANES)
            part[at, :, columns] = jnp.transpose(conc[:, at, columns], (1, 0, 2))
        return carry

    lax.fori_loop(0, depth // TILE, turn_rows, 0)

    def pad_row(d, carry):
        x_blocks = [part[d, :, j * LANES : (j + 1) * LANES] for j in range(blocks)]
        turned = [pltpu.roll(block, LANES - 1, 1) for block in x_blocks]

        def lane_of(block, at):
            return jnp.broadcast_to(block[:, at : at + 1], (TILE, LANES))

        first, second = lane_of(x_blocks[0], 0), lane_of(x_blocks[0], 1)
        before_last, last = lane_of(x_blocks[-1], LANES - 2), lane_of(x_blocks[-1], LANES - 1)
        pad_left[d, 0] = first
        pad_step[d, 0] = second - first
        for j in range(blocks):
            if j < blocks - 1:
                left = x_blocks[j]
                right = jnp.where(lane == LANES - 1, turned[j + 1], turned[j])
            else:
                left = jnp.where(lane == LANES - 1, before_last, x_blocks[j])
                right = jnp.where(lane == LANES - 1, last, turned[j])
            pad_left[d, j + 1] = left
            pad_step[d, j + 1] = right - left
        for j in (blocks + 1, blocks + 2):
            pad_left[d, j] = before_last
            pad_step[d, j] = last - before_last
        return carry

    lax.fori_loop(0, depth, pad_row, 0, unroll=4)

    for fetch in fetches[1:3]:
        fetch.wait()

    for v in range(views):

        def take_row(d, row, shares, sums):
            start = start_of(v, d)
            block, rest = start >> 7, start & (LANES - 1)
            turn = (LANES - rest) & (LANES - 1)
            left = pltpu.roll(pad_left[d, pl.ds(block, blocks + 1)], turn, 2)
            step = pltpu.roll(pad_step[d, pl.ds(block, blocks + 1)], turn, 2)
            whole = lane < LANES - rest
            new = []
            for j in range(blocks):
                at = pl.ds(j * LANES, LANES)
                share = jnp.broadcast_to(shares[row : row + 1, j * LANES : (j + 1) * LANES], (TILE, LANES))
                value = jnp.where(whole, left[j], left[j + 1]) + share * jnp.where(whole, step[j], step[j + 1])
                field[v, pl.ds(pl.multiple_of(d * TILE, TILE), TILE), at] = value
                new.append(sums[j] + value)
            return tuple(new)

        def take_rows(i, sums):
            base = pl.multiple_of(i * TILE, TILE)
            shares = weight[v, pl.ds(base, TILE), :]
            for row in range(TILE):
                sums = take_row(base + row, row, shares, sums)
            return sums

        zero = jnp.zeros((TILE, LANES), F32)
        sums = lax.fori_loop(0, depth // TILE, take_rows, (zero,) * blocks)
        for j in range(0, blocks, 2):
            chunk, offset = divmod(v * blocks + j, tiles)
            levels = [
                jnp.sum(att_tile[k] * sums[j + h], axis=0, keepdims=True) for h in range(2) for k in range(4)
            ]
            slab[chunk, tiles + offset // 2] = stack_rows(levels)

    pl.semaphore_wait(barrier, greeted)

    def to_group(k):
        return pltpu.make_async_remote_copy(
            src_ref=slab.at[k],
            dst_ref=group.at[c],
            send_sem=send1.at[0],
            recv_sem=recv1.at[0],
            device_id={"depth": in_group(k)},
            device_id_type=MESH,
        )

    def emit_chunk(chunk):
        v, base = chunk // per_view, (chunk % per_view) * wide
        for part_at in range(0, wide, STEP):
            at = pl.ds(pl.multiple_of(base + part_at, STEP), STEP)
            values = field[v, :, at]
            value = jnp.exp(-dot3(mat_high, mat_low, values))
            decay[v, :, at] = value
            value = (value * values).reshape(depth, TILE, STEP)
            value = jnp.sum(value, axis=0)
            for j in range(STEP // LANES):
                slab[chunk, part_at // LANES + j] = value[:, j * LANES : (j + 1) * LANES] * yield_tile

    def emit(i, carry):
        chunks = [flip(nc - PAIR * (i + 1) + k) for k in range(PAIR)]
        for chunk in chunks:
            emit_chunk(chunk)
        for chunk in chunks:

            @pl.when(chunk != c)
            def _():
                to_group(chunk).start()

        return carry

    lax.fori_loop(0, nc // PAIR, emit, 0)
    group[c] = slab[c]

    all_of(group.at[: nc - 1], recv1.at[0]).wait_recv()

    line_wide = over(line_tile, wide)

    def scales(ref, count):
        first, later = [], []
        for j in range(count):
            levels = [
                jnp.concatenate([packed_row(ref, j, b, k) for b in range(tiles)], axis=1) for k in range(4)
            ]
            first.append(levels[0])
            later.append(pick(line_wide, levels[1:]))
        after = [None] * count
        run = jnp.zeros((TILE, wide), F32)
        for j in reversed(range(count)):
            after[j] = run
            run = run + later[j]
        result = []
        run = jnp.zeros((TILE, wide), F32)
        for j in range(count):
            result.append(jnp.exp(-(run + after[j])))
            run = run + first[j]
        return result

    emitted_sum = jnp.zeros((TILE, wide), F32)
    for j, scale in enumerate(scales(group, nc)):
        piece = columns_of(group, j) * scale
        local_scale[j] = scale
        local_part[j] = piece
        emitted_sum += piece
    for b in range(tiles):
        group_send[b] = emitted_sum[:, b * LANES : (b + 1) * LANES]
    for b in range(tiles, tiles + tiles // 2):
        value = group[0, b]
        for j in range(1, nc):
            value = value + group[j, b]
        group_send[b] = value

    def y_copy(peer, slot):
        return pltpu.make_async_remote_copy(
            src_ref=group_send,
            dst_ref=group_recv.at[slot],
            send_sem=send2.at[0],
            recv_sem=recv2.at[0],
            device_id={"depth": in_y(peer)},
            device_id_type=MESH,
        )

    for k in sorted(range(1, ny), key=lambda k: -min(k, ny - k)):
        y_copy((y + k) % ny, y).start()
    group_recv[y] = group_send[...]
    all_of(group_recv.at[: ny - 1], recv2.at[0]).wait_recv()

    total = jnp.zeros((TILE, wide), F32)
    prior = jnp.zeros((TILE, wide), F32)
    following = jnp.zeros((TILE, wide), F32)
    for j, scale in enumerate(scales(group_recv, ny)):
        piece = columns_of(group_recv, j) * scale
        group_scale[j] = scale
        total += piece
        prior += jnp.where(j < y, piece, 0.0)
        following += jnp.where(j > y, piece, 0.0)
    pltpu.make_async_copy(measured, measured, fetched.at[6]).wait()
    counts = total * (1.0 / depth_total)
    misfit = counts - jnp.concatenate([measured[e] for e in range(TILE)], axis=0)
    here_scale = group_scale[y]
    later = [None] * nc
    run = following
    for j in reversed(range(nc)):
        later[j] = jnp.sum(misfit * run, axis=0, keepdims=True)
        run = run + local_part[j] * here_scale
    run = prior
    yield_wide = over(yield_tile, wide)
    for j in range(nc):
        value = misfit * yield_wide * local_scale[j] * here_scale
        for b in range(tiles):
            back[j, b] = value[:, b * LANES : (b + 1) * LANES]
        mixed = misfit * run
        levels = [later[j]] + [
            jnp.sum(jnp.where(line_wide == k, mixed, 0.0), axis=0, keepdims=True) for k in range(3)
        ]
        for b in range(0, tiles, 2):
            back[j, tiles + b // 2] = stack_rows(
                [level[:, (b + h) * LANES : (b + h + 1) * LANES] for h in range(2) for level in levels]
            )
        run = run + local_part[j] * here_scale

    def seed_copy(peer, slot):
        return pltpu.make_async_remote_copy(
            src_ref=back.at[peer],
            dst_ref=seeds.at[slot],
            send_sem=send3.at[0],
            recv_sem=recv3.at[slot],
            device_id={"depth": in_group(peer)},
            device_id_type=MESH,
        )

    def total_copy(peer, slot):
        at = pl.ds(pl.multiple_of((slot % per_view) * wide, LANES), wide)
        return pltpu.make_async_remote_copy(
            src_ref=total_send,
            dst_ref=signal.at[slot // per_view, :, :, at],
            send_sem=send4.at[0],
            recv_sem=recv4.at[0],
            device_id={"depth": in_group(peer)},
            device_id_type=MESH,
        )

    for k in reversed(range(1, nc)):
        seed_copy(flip(k), c).start()
    seeds[c] = back[c]
    for e in range(TILE):
        total_send[e] = counts[e : e + 1]
        signal[own_view, e, :, own_at] = counts[e : e + 1]
    for k in range(1, nc):
        total_copy((c + k) % nc, c).start()

    def clear(d, carry):
        zeros = jnp.zeros((3, TILE, LANES), F32)
        for v in range(views):
            spread_left[v, d, 0:3] = zeros
            spread_right[v, d, 0:3] = zeros
            spread_left[v, d, 3 + blocks : 5 + blocks] = zeros[:2]
            spread_right[v, d, 3 + blocks : 5 + blocks] = zeros[:2]
        return carry

    lax.fori_loop(0, depth, clear, 0)

    def adjoint_chunk(chunk, corr):
        v, base = chunk // per_view, (chunk % per_view) * wide
        for part_at in range(0, wide, STEP):
            start = pl.multiple_of(base + part_at, STEP)
            at = pl.ds(start, STEP)
            here = range(part_at // LANES, (part_at + STEP) // LANES)
            factor = jnp.concatenate([seeds[chunk, b] for b in here], axis=1)
            constant = jnp.concatenate(
                [sum(att_tile[k] * packed_row(seeds, chunk, b, k) for k in range(4)) for b in here], axis=1
            )
            direct = decay[v, :, at].reshape(depth, TILE, STEP) * factor[None]
            mixed = direct.reshape(depth * TILE, STEP) * field[v, :, at]
            corr[...] = dot3(adj_high, adj_low, mixed)
            for d in range(depth):
                if d % TILE == 0:
                    shares = weight[v, d : d + TILE, at]
                rows = slice(d * TILE, (d + 1) * TILE)
                value = decay[v, rows, at] * factor - corr[rows, :] - constant
                right = value * jnp.broadcast_to(shares[d % TILE : d % TILE + 1], (TILE, STEP))
                left = value - right
                rest = start_of(v, d) & (LANES - 1)
                for j in range(STEP // LANES):
                    to = 3 + start // LANES + j
                    spread_left[v, d, to] = pltpu.roll(left[:, j * LANES : (j + 1) * LANES], rest, 1)
                    spread_right[v, d, to] = pltpu.roll(right[:, j * LANES : (j + 1) * LANES], rest, 1)

    def adjoint(i, carry):
        chunks = [flip(PAIR * i + k) for k in range(PAIR)]
        for chunk in chunks:

            @pl.when(chunk != c)
            def _():
                seed_copy(chunk, chunk).wait_recv()

        for k, chunk in enumerate(chunks):
            adjoint_chunk(chunk, corr.at[k])
        return carry

    lax.fori_loop(0, nc // PAIR, adjoint, 0)

    share_x = depth // nx
    share_z = share_x // nz
    share = share_z // SPLIT

    def row_of(px, pz, s):
        return px * share_x + pz * share_z + s * share

    def x_copy(k, pz, s):
        peer = (x + k) % nx
        return pltpu.make_async_remote_copy(
            src_ref=part.at[pl.ds(row_of(peer, pz, s), share)],
            dst_ref=from_x.at[pz, s, k - 1],
            send_sem=send5.at[0],
            recv_sem=recv5.at[pz, s],
            device_id={"views": in_x(peer)},
            device_id_type=MESH,
        )

    def place(i, carry):
        pz, s = (zh + 1 + i // SPLIT) % nz, i % SPLIT
        for d in [row_of((x + 1 + k) % nx, pz, s) + r for k in range(nx) for r in range(share)]:
            lefts = [None] * (blocks + 2)
            rights = [None] * (blocks + 2)
            for v in range(views):
                start = start_of(v, d)
                block, rest = start >> 7, start & (LANES - 1)
                for ref, sums in ((spread_left, lefts), (spread_right, rights)):
                    turned = ref[v, d, pl.ds(2 - block, blocks + 3)]
                    for j in range(blocks + 2):
                        value = jnp.where(lane >= rest, turned[j + 1], turned[j])
                        sums[j] = value if v == 0 else sums[j] + value

            def total_of(value):
                return jnp.sum(value, axis=1, keepdims=True)

            low_left, low_right = total_of(lefts[0]), total_of(rights[0])
            top = lane == LANES - 1
            high_left = total_of(lefts[-1] + jnp.where(top, lefts[-2], 0.0))
            high_right = total_of(rights[-1])
            shifted = [pltpu.roll(rights[j + 1], 1, 1) for j in range(blocks)]
            for j in range(blocks):
                left = lefts[j + 1]
                if j == 0:
                    right = jnp.where(lane == 0, 0.0, shifted[0])
                    left = left + jnp.where(lane == 0, low_left, 0.0) + jnp.where(lane == 1, low_right, 0.0)
                else:
                    right = jnp.where(lane == 0, shifted[j - 1], shifted[j])
                if j == blocks - 1:
                    left = jnp.where(top, high_right + rights[-2], left)
                    left = left + jnp.where(lane == LANES - 2, high_left, 0.0)
                part[d, :, j * LANES : (j + 1) * LANES] = left + right

        for k in range(1, nx):
            x_copy(k, pz, s).start()
        return carry

    lax.fori_loop(0, nz * SPLIT, place, 0)

    def reduce_x(pz, s):
        all_of(from_x.at[pz, s], recv5.at[pz, s]).wait_recv()
        for r in range(share):
            value = part[row_of(x, pz, s) + r]
            for k in range(1, nx):
                value = value + from_x[pz, s, k - 1, r]
            z_out[pz, s, r] = value

    def z_copy(peer, s, slot):
        return pltpu.make_async_remote_copy(
            src_ref=z_out.at[peer, s],
            dst_ref=from_z.at[slot, s],
            send_sem=send6.at[0],
            recv_sem=recv6.at[slot, s],
            device_id={"views": in_z(peer)},
            device_id_type=MESH,
        )

    def piece(px, pz, s):
        return full.at[pl.ds(row_of(px, pz, s), share)]

    def give_x(step, px, pz, s):
        return pltpu.make_async_remote_copy(
            src_ref=piece(px, pz, s),
            dst_ref=piece(px, pz, s),
            send_sem=send7.at[0],
            recv_sem=recv7.at[px, pz, s],
            device_id={"views": in_x((x + step) % nx)},
            device_id_type=MESH,
        )

    def give_z(peer, px, pz, s):
        return pltpu.make_async_remote_copy(
            src_ref=piece(px, pz, s),
            dst_ref=piece(px, pz, s),
            send_sem=send8.at[0],
            recv_sem=recv7.at[px, pz, s],
            device_id={"views": in_z(peer)},
            device_id_type=MESH,
        )

    for s in range(SPLIT):
        for k in range(1, nz):
            reduce_x((zh + k) % nz, s)
            z_copy((zh + k) % nz, s, zh).start()

    steps = [1] if nx == 2 else [1, nx - 1]
    waited = set()

    def spread_x(pz, s):
        for step in steps:
            give_x(step, x, pz, s).start()

    def receive(step, turn, s):
        px, pz = (x + step) % nx, (zh + turn) % nz
        give_x(0, px, pz, s).wait_recv()
        waited.add((step, turn, s))
        return px, pz

    def relay(turn, s):
        if nx == 4:
            onward = 1 if s % 2 == 0 else nx - 1
            px, pz = receive(nx - onward, turn, s)
            give_x(onward, px, pz, s).start()

    for s in range(SPLIT):
        reduce_x(zh, s)
        for k in range(1, nz):
            z_copy((zh + k) % nz, s, (zh + k) % nz).wait_recv()
        for r in range(share):
            value = z_out[zh, s, r]
            for k in range(1, nz):
                value = value + from_z[(zh + k) % nz, s, r]
            full[row_of(x, zh, s) + r] = value
        for k in range(1, nz):
            give_z((zh + k) % nz, x, zh, s).start()
        spread_x(zh, s)
    for s in range(SPLIT):
        relay(0, s)
        for k in range(1, nz):
            _, pz = receive(0, k, s)
            spread_x(pz, s)
    for k in range(1, nz):
        for s in range(SPLIT):
            relay(k, s)
    def turn_out(px):
        for o in range(share_x // TILE):
            at = pl.ds(pl.multiple_of(px * share_x + o * TILE, TILE), TILE)
            for j in range(blocks):
                columns = slice(j * LANES, (j + 1) * LANES)
                grad[:, at, columns] = jnp.transpose(full[at, :, columns], (1, 0, 2))

    turn_out(x)
    for step in [1, nx - 1, 2][: nx - 1]:
        for k in range(nz):
            for s in range(SPLIT):
                if (step, k, s) not in waited:
                    receive(step, k, s)
        turn_out((x + step) % nx)

    all_of(signal.at[:, : nc - 1], recv4.at[0]).wait_recv()
    all_of(slab.at[: nc - 1], send1.at[0]).wait_send()
    all_of(group_recv.at[: ny - 1], send2.at[0]).wait_send()
    all_of(back.at[: nc - 1], send3.at[0]).wait_send()
    all_of(signal.at[:, : nc - 1], send4.at[0]).wait_send()
    all_of(part.at[: (nx - 1) * share_x], send5.at[0]).wait_send()
    all_of(z_out.at[: nz - 1], send6.at[0]).wait_send()
    all_of(full.at[: (nx - 1) * share_x], send7.at[0]).wait_send()
    all_of(z_out.at[: nz - 1], send8.at[0]).wait_send()


def body(sizes, concentration, shear_index, shear_weight, attenuation, yields, line_energy, measured):
    elements, rows, depth, width = concentration.shape
    views = shear_index.shape[0]
    nx, nz, ny, nc = sizes
    wide = views * width // nc
    tiles = wide // LANES
    blocks = width // LANES
    share = depth // nx // nz // SPLIT
    hbm = pl.BlockSpec(memory_space=pltpu.HBM)
    vmem = pl.BlockSpec(memory_space=pltpu.VMEM)
    full = depth * elements

    def buf(*shape):
        return pltpu.VMEM(shape, F32)

    def sems(*shape):
        return pltpu.SemaphoreType.DMA(shape)

    gradient, signal = pl.pallas_call(
        functools.partial(kernel, sizes),
        out_shape=(
            pltpu.VMEM((elements, depth, width), F32),
            pltpu.VMEM((views, elements, rows, width), F32),
        ),
        in_specs=[hbm] * 7,
        out_specs=(vmem, vmem),
        scratch_shapes=[
            pltpu.SMEM((views, depth, LANES), jnp.int32),
            pltpu.SMEM(attenuation.shape, F32),
            pltpu.SMEM(yields.shape, F32),
            pltpu.SMEM(line_energy.shape, jnp.int32),
            buf(elements, depth, width),
            buf(views, depth, width),
            buf(elements, rows, wide),
            sems(7),
        ]
        + [pltpu.VMEM((full, full), BF16)] * 4
        + [buf(depth, blocks + 3, elements, LANES)] * 2
        + [buf(views, full, width)] * 2
        + [buf(views, depth, blocks + 5, elements, LANES)] * 2
        + [
            buf(PAIR, full, STEP),
            buf(nc, tiles + tiles // 2, elements, LANES),
            buf(nc, tiles + tiles // 2, elements, LANES),
            buf(nc, elements, wide),
            buf(nc, elements, wide),
            buf(tiles + tiles // 2, elements, LANES),
            buf(ny, tiles + tiles // 2, elements, LANES),
            buf(ny, elements, wide),
            buf(nc, tiles + tiles // 2, elements, LANES),
            buf(nc, tiles + tiles // 2, elements, LANES),
            buf(elements, rows, wide),
            buf(depth, elements, width),
            buf(nz, SPLIT, nx - 1, share, elements, width),
            buf(nz, SPLIT, share, elements, width),
            buf(nz, SPLIT, share, elements, width),
            buf(depth, elements, width),
        ]
        + [sems(1)] * 5
        + [sems(nc)]
        + [sems(1)] * 3
        + [sems(nz, SPLIT), sems(1), sems(nz, SPLIT)]
        + [sems(1), sems(nx, nz, SPLIT), sems(1)],
        compiler_params=pltpu.CompilerParams(
            collective_id=0, has_side_effects=True, vmem_limit_bytes=56 * 1024 * 1024
        ),
    )(
        shear_index,
        attenuation,
        yields,
        line_energy,
        concentration.reshape(elements, depth, width),
        shear_weight,
        measured,
    )
    return gradient.reshape(elements, rows, depth, width), signal


SIZES = {(8, 64): (4, 2, 8, 8)}


def solution(mesh):
    sizes = SIZES[mesh.shape["views"], mesh.shape["depth"]]
    return jax.shard_map(
        functools.partial(body, sizes),
        mesh=mesh,
        in_specs=(
            P(None, None, "depth", None),
            P("views", "depth", None),
            P("views", "depth", None),
            P(),
            P(),
            P(),
            P("views", None, None, None),
        ),
        out_specs=(P(None, None, "depth", None), P("views", None, None, None)),
        check_vma=False,
    )
```

```python
import functools

import jax
import jax.numpy as jnp
from jax import lax
from jax.experimental import pallas as pl
from jax.experimental.pallas import tpu as pltpu
from jax.sharding import PartitionSpec as P

LANES = 128
TILE = 8
STEP = 256
PAIR = 4
HALVES = 1
MESH = pl.DeviceIdType.MESH
F32 = jnp.float32
BF16 = jnp.bfloat16


def split(value):
    high = value.astype(BF16)
    low = (value - high.astype(F32)).astype(BF16)
    return high, low


def dot3(high_ref, low_ref, right):
    right_high, right_low = split(right)
    high = high_ref[...]
    result = jnp.dot(high, right_high, preferred_element_type=F32)
    result += jnp.dot(high, right_low, preferred_element_type=F32)
    return result + jnp.dot(low_ref[...], right_high, preferred_element_type=F32)


def kernel(
    sizes,
    index_in,
    att_in,
    yields_in,
    line_in,
    conc_in,
    weight_in,
    measured_in,
    grad,
    signal,
    shifts,
    att,
    yields,
    line,
    conc,
    weight,
    measured,
    fetched,
    mat_high,
    mat_low,
    adj_high,
    adj_low,
    pad_left,
    pad_step,
    field,
    decay,
    spread_left,
    spread_right,
    corr,
    slab,
    group,
    local_scale,
    local_part,
    group_send,
    group_recv,
    group_scale,
    back,
    seeds,
    total_send,
    part,
    from_x,
    z_out,
    from_z,
    full,
    send1,
    recv1,
    send2,
    recv2,
    send3,
    recv3,
    send4,
    recv4,
    send5,
    recv5,
    send6,
    recv6,
    send7,
    recv7,
    send8,
    recv8,
    recv9,
):
    nx, nz, ny, nc = sizes
    views, depth, width = weight.shape
    blocks = width // LANES
    wide = views * width // nc
    per_view = width // wide
    tiles = wide // LANES
    depth_total = depth * ny * nc
    vi, di = lax.axis_index("views"), lax.axis_index("depth")
    x, zh = vi // nz, vi % nz
    y, c = di // nc, di % nc

    def flip(k):
        bits = [((c // b + k // b) % 2) * b for b in (1, 2, 4) if b < nc]
        return sum(bits)

    def in_group(k):
        return y * nc + k

    def in_y(k):
        return k * nc + c

    def in_x(k):
        return k * nz + zh

    def in_z(k):
        return x * nz + k

    own_view, own_base = c // per_view, pl.multiple_of((c % per_view) * wide, LANES)
    own_at = pl.ds(own_base, wide)
    middle = width // 2
    fetches = [
        pltpu.make_async_copy(src, dst, fetched.at[min(i, 6)])
        for i, (src, dst) in enumerate(
            [
                (conc_in, conc),
                (weight_in, weight),
                (index_in.at[:, :, middle : middle + LANES], shifts),
                (att_in, att),
                (yields_in, yields),
                (line_in, line),
            ]
            + [(measured_in.at[own_view, e, :, own_at], measured.at[e]) for e in range(TILE)]
        )
    ]
    for fetch in fetches:
        fetch.start()

    def start_of(v, d):
        return jnp.clip(shifts[v, d, 0] - (middle - LANES), 0, 2 * LANES)

    def all_of(ref, sem):
        return pltpu.make_async_remote_copy(
            src_ref=ref,
            dst_ref=ref,
            send_sem=sem,
            recv_sem=sem,
            device_id={"depth": in_group(flip(1))},
            device_id_type=MESH,
        )

    barrier = pltpu.get_barrier_semaphore()
    greeted = 0
    for k in range(1, nc):
        pl.semaphore_signal(barrier, inc=1, device_id={"depth": in_group((c + k) % nc)}, device_id_type=MESH)
        greeted += 1
    for k in range(1, ny):
        pl.semaphore_signal(barrier, inc=1, device_id={"depth": in_y((y + k) % ny)}, device_id_type=MESH)
        greeted += 1
    for k in range(1, nx):
        pl.semaphore_signal(barrier, inc=1, device_id={"views": in_x((x + k) % nx)}, device_id_type=MESH)
        greeted += 1
    for k in range(1, nz):
        pl.semaphore_signal(barrier, inc=1, device_id={"views": in_z((zh + k) % nz)}, device_id_type=MESH)
        greeted += 1

    for fetch in fetches[3:6]:
        fetch.wait()

    rows16 = lax.broadcasted_iota(jnp.int32, (2 * TILE, depth * TILE), 0)
    cols16 = lax.broadcasted_iota(jnp.int32, (2 * TILE, depth * TILE), 1)
    row_item, col_item, col_depth = rows16 & (TILE - 1), cols16 & (TILE - 1), cols16 // TILE

    def spread(item, values):
        result = jnp.full(item.shape, values[0])
        for i in range(1, TILE):
            result = jnp.where(item == i, values[i], result)
        return result

    att_col = [spread(col_item, [att[k, e] for e in range(TILE)]) for k in range(4)]
    att_row = [spread(row_item, [att[k, e] for e in range(TILE)]) for k in range(4)]
    line_col = spread(col_item, [line[e] for e in range(TILE)])
    line_row = spread(row_item, [line[e] for e in range(TILE)])

    def pick(which, options):
        return jnp.where(which == 0, options[0], jnp.where(which == 1, options[1], options[2]))

    forward_out = pick(line_row, att_col[1:])
    adjoint_out = pick(line_col, att_row[1:])
    for i in range(depth // 2):
        here = rows16 // TILE + 2 * i
        rows = pl.ds(2 * TILE * i, 2 * TILE)
        mat = jnp.where(col_depth < here, att_col[0], jnp.where(col_depth > here, forward_out, 0.0))
        mat_high[rows, :], mat_low[rows, :] = split(mat)
        adj = jnp.where(col_depth > here, att_row[0], jnp.where(col_depth < here, adjoint_out, 0.0))
        adj_high[rows, :], adj_low[rows, :] = split(adj)
    att_tile = [value[:TILE, :LANES] for value in att_row]
    line_tile = line_row[:TILE, :LANES]
    yield_tile = spread(row_item[:TILE, :LANES], [yields[e] for e in range(TILE)])

    def over(tile, columns):
        return jnp.concatenate([tile] * (columns // LANES), axis=1)

    lane = lax.broadcasted_iota(jnp.int32, (TILE, LANES), 1)
    sub = lax.broadcasted_iota(jnp.int32, (TILE, LANES), 0)

    def stack_rows(levels):
        result = jnp.broadcast_to(levels[0], (TILE, LANES))
        for k in range(1, TILE):
            result = jnp.where(sub == k, jnp.broadcast_to(levels[k], (TILE, LANES)), result)
        return result

    def columns_of(ref, j):
        return jnp.concatenate([ref[j, b] for b in range(tiles)], axis=1)

    def packed_row(ref, j, b, k):
        at = 4 * (b % 2) + k
        return jnp.broadcast_to(ref[j, tiles + b // 2, at : at + 1, :], (TILE, LANES))

    fetches[0].wait()

    def turn_rows(i, carry):
        at = pl.ds(pl.multiple_of(i * TILE, TILE), TILE)
        for j in range(blocks):
            columns = slice(j * LANES, (j + 1) * LANES)
            part[at, :, columns] = jnp.transpose(conc[:, at, columns], (1, 0, 2))
        return carry

    lax.fori_loop(0, depth // TILE, turn_rows, 0, unroll=True)

    def pad_row(d, carry):
        x_blocks = [part[d, :, j * LANES : (j + 1) * LANES] for j in range(blocks)]
        turned = [pltpu.roll(block, LANES - 1, 1) for block in x_blocks]

        def lane_of(block, at):
            return jnp.broadcast_to(block[:, at : at + 1], (TILE, LANES))

        first, second = lane_of(x_blocks[0], 0), lane_of(x_blocks[0], 1)
        before_last, last = lane_of(x_blocks[-1], LANES - 2), lane_of(x_blocks[-1], LANES - 1)
        pad_left[d, 0] = first
        pad_step[d, 0] = second - first
        for j in range(blocks):
            if j < blocks - 1:
                left = x_blocks[j]
                right = jnp.where(lane == LANES - 1, turned[j + 1], turned[j])
            else:
                left = jnp.where(lane == LANES - 1, before_last, x_blocks[j])
                right = jnp.where(lane == LANES - 1, last, turned[j])
            pad_left[d, j + 1] = left
            pad_step[d, j + 1] = right - left
        for j in (blocks + 1, blocks + 2):
            pad_left[d, j] = before_last
            pad_step[d, j] = last - before_last
        return carry

    lax.fori_loop(0, depth, pad_row, 0, unroll=8)

    for fetch in fetches[1:3]:
        fetch.wait()

    for v in range(views):

        def take_row(d, row, shares, sums):
            start = start_of(v, d)
            block, rest = start >> 7, start & (LANES - 1)
            turn = (LANES - rest) & (LANES - 1)
            left = pltpu.roll(pad_left[d, pl.ds(block, blocks + 1)], turn, 2)
            step = pltpu.roll(pad_step[d, pl.ds(block, blocks + 1)], turn, 2)
            whole = lane < LANES - rest
            new = []
            for j in range(blocks):
                at = pl.ds(j * LANES, LANES)
                share = jnp.broadcast_to(shares[row : row + 1, j * LANES : (j + 1) * LANES], (TILE, LANES))
                value = jnp.where(whole, left[j], left[j + 1]) + share * jnp.where(whole, step[j], step[j + 1])
                field[v, pl.ds(pl.multiple_of(d * TILE, TILE), TILE), at] = value
                new.append(sums[j] + value)
            return tuple(new)

        def take_rows(i, sums):
            base = pl.multiple_of(i * TILE, TILE)
            shares = weight[v, pl.ds(base, TILE), :]
            for row in range(TILE):
                sums = take_row(base + row, row, shares, sums)
            return sums

        zero = jnp.zeros((TILE, LANES), F32)
        sums = lax.fori_loop(0, depth // TILE, take_rows, (zero,) * blocks, unroll=2)
        for j in range(0, blocks, 2):
            chunk, offset = divmod(v * blocks + j, tiles)
            levels = [
                jnp.sum(att_tile[k] * sums[j + h], axis=0, keepdims=True) for h in range(2) for k in range(4)
            ]
            slab[chunk, tiles + offset // 2] = stack_rows(levels)

    pl.semaphore_wait(barrier, greeted)

    def to_group(k):
        return pltpu.make_async_remote_copy(
            src_ref=slab.at[k],
            dst_ref=group.at[c],
            send_sem=send1.at[0],
            recv_sem=recv1.at[0],
            device_id={"depth": in_group(k)},
            device_id_type=MESH,
        )

    def emit_chunk(chunk):
        v, base = chunk // per_view, (chunk % per_view) * wide
        for part_at in range(0, wide, STEP):
            at = pl.ds(pl.multiple_of(base + part_at, STEP), STEP)
            values = field[v, :, at]
            value = jnp.exp(-dot3(mat_high, mat_low, values))
            decay[v, :, at] = value
            value = (value * values).reshape(depth, TILE, STEP)
            value = jnp.sum(value, axis=0)
            for j in range(STEP // LANES):
                slab[chunk, part_at // LANES + j] = value[:, j * LANES : (j + 1) * LANES] * yield_tile

    def emit(i, carry):
        chunks = [flip(nc - PAIR * (i + 1) + k) for k in range(PAIR)]
        for chunk in chunks:
            emit_chunk(chunk)
        for chunk in chunks:

            @pl.when(chunk != c)
            def _():
                to_group(chunk).start()

        return carry

    lax.fori_loop(0, nc // PAIR, emit, 0)
    group[c] = slab[c]

    all_of(group.at[: nc - 1], recv1.at[0]).wait_recv()

    line_wide = over(line_tile, wide)

    def scales(ref, count):
        first, later = [], []
        for j in range(count):
            levels = [
                jnp.concatenate([packed_row(ref, j, b, k) for b in range(tiles)], axis=1) for k in range(4)
            ]
            first.append(levels[0])
            later.append(pick(line_wide, levels[1:]))
        after = [None] * count
        run = jnp.zeros((TILE, wide), F32)
        for j in reversed(range(count)):
            after[j] = run
            run = run + later[j]
        result = []
        run = jnp.zeros((TILE, wide), F32)
        for j in range(count):
            result.append(jnp.exp(-(run + after[j])))
            run = run + first[j]
        return result

    emitted_sum = jnp.zeros((TILE, wide), F32)
    for j, scale in enumerate(scales(group, nc)):
        piece = columns_of(group, j) * scale
        local_scale[j] = scale
        local_part[j] = piece
        emitted_sum += piece
    for b in range(tiles):
        group_send[b] = emitted_sum[:, b * LANES : (b + 1) * LANES]
    for b in range(tiles, tiles + tiles // 2):
        value = group[0, b]
        for j in range(1, nc):
            value = value + group[j, b]
        group_send[b] = value

    def y_copy(peer, slot):
        return pltpu.make_async_remote_copy(
            src_ref=group_send,
            dst_ref=group_recv.at[slot],
            send_sem=send2.at[0],
            recv_sem=recv2.at[0],
            device_id={"depth": in_y(peer)},
            device_id_type=MESH,
        )

    for k in sorted(range(1, ny), key=lambda k: -min(k, ny - k)):
        y_copy((y + k) % ny, y).start()
    group_recv[y] = group_send[...]
    all_of(group_recv.at[: ny - 1], recv2.at[0]).wait_recv()

    total = jnp.zeros((TILE, wide), F32)
    prior = jnp.zeros((TILE, wide), F32)
    following = jnp.zeros((TILE, wide), F32)
    for j, scale in enumerate(scales(group_recv, ny)):
        piece = columns_of(group_recv, j) * scale
        group_scale[j] = scale
        total += piece
        prior += jnp.where(j < y, piece, 0.0)
        following += jnp.where(j > y, piece, 0.0)
    pltpu.make_async_copy(measured, measured, fetched.at[6]).wait()
    counts = total * (1.0 / depth_total)
    misfit = counts - jnp.concatenate([measured[e] for e in range(TILE)], axis=0)
    here_scale = group_scale[y]
    later = [None] * nc
    run = following
    for j in reversed(range(nc)):
        later[j] = jnp.sum(misfit * run, axis=0, keepdims=True)
        run = run + local_part[j] * here_scale
    run = prior
    yield_wide = over(yield_tile, wide)
    for j in range(nc):
        value = misfit * yield_wide * local_scale[j] * here_scale
        for b in range(tiles):
            back[j, b] = value[:, b * LANES : (b + 1) * LANES]
        mixed = misfit * run
        levels = [later[j]] + [
            jnp.sum(jnp.where(line_wide == k, mixed, 0.0), axis=0, keepdims=True) for k in range(3)
        ]
        for b in range(0, tiles, 2):
            back[j, tiles + b // 2] = stack_rows(
                [level[:, (b + h) * LANES : (b + h + 1) * LANES] for h in range(2) for level in levels]
            )
        run = run + local_part[j] * here_scale

    def seed_copy(peer, slot):
        return pltpu.make_async_remote_copy(
            src_ref=back.at[peer],
            dst_ref=seeds.at[slot],
            send_sem=send3.at[0],
            recv_sem=recv3.at[slot],
            device_id={"depth": in_group(peer)},
            device_id_type=MESH,
        )

    def total_copy(peer, slot):
        at = pl.ds(pl.multiple_of((slot % per_view) * wide, LANES), wide)
        return pltpu.make_async_remote_copy(
            src_ref=total_send,
            dst_ref=signal.at[slot // per_view, :, :, at],
            send_sem=send4.at[0],
            recv_sem=recv4.at[0],
            device_id={"depth": in_group(peer)},
            device_id_type=MESH,
        )

    for k in reversed(range(1, nc)):
        seed_copy(flip(k), c).start()
    seeds[c] = back[c]
    for e in range(TILE):
        total_send[e] = counts[e : e + 1]
        signal[own_view, e, :, own_at] = counts[e : e + 1]
    for k in range(1, nc):
        total_copy((c + k) % nc, c).start()

    def clear(d, carry):
        zeros = jnp.zeros((3, TILE, LANES), F32)
        for v in range(views):
            spread_left[v, d, 0:3] = zeros
            spread_right[v, d, 0:3] = zeros
            spread_left[v, d, 3 + blocks : 5 + blocks] = zeros[:2]
            spread_right[v, d, 3 + blocks : 5 + blocks] = zeros[:2]
        return carry

    lax.fori_loop(0, depth, clear, 0)

    def adjoint_chunk(chunk, corr):
        v, base = chunk // per_view, (chunk % per_view) * wide
        for part_at in range(0, wide, STEP):
            start = pl.multiple_of(base + part_at, STEP)
            at = pl.ds(start, STEP)
            here = range(part_at // LANES, (part_at + STEP) // LANES)
            factor = jnp.concatenate([seeds[chunk, b] for b in here], axis=1)
            constant = jnp.concatenate(
                [sum(att_tile[k] * packed_row(seeds, chunk, b, k) for k in range(4)) for b in here], axis=1
            )
            direct = decay[v, :, at].reshape(depth, TILE, STEP) * factor[None]
            mixed = direct.reshape(depth * TILE, STEP) * field[v, :, at]
            corr[...] = dot3(adj_high, adj_low, mixed)
            for d in range(depth):
                if d % TILE == 0:
                    shares = weight[v, d : d + TILE, at]
                rows = slice(d * TILE, (d + 1) * TILE)
                value = decay[v, rows, at] * factor - corr[rows, :] - constant
                right = value * jnp.broadcast_to(shares[d % TILE : d % TILE + 1], (TILE, STEP))
                left = value - right
                rest = start_of(v, d) & (LANES - 1)
                for j in range(STEP // LANES):
                    to = 3 + start // LANES + j
                    spread_left[v, d, to] = pltpu.roll(left[:, j * LANES : (j + 1) * LANES], rest, 1)
                    spread_right[v, d, to] = pltpu.roll(right[:, j * LANES : (j + 1) * LANES], rest, 1)

    def adjoint(i, carry):
        chunks = [flip(PAIR * i + k) for k in range(PAIR)]
        for chunk in chunks:

            @pl.when(chunk != c)
            def _():
                seed_copy(chunk, chunk).wait_recv()

        for k, chunk in enumerate(chunks):
            adjoint_chunk(chunk, corr.at[k])
        return carry

    lax.fori_loop(0, nc // PAIR, adjoint, 0)

    share_x = depth // nx
    share_z = share_x // nz
    pieces = share_z * HALVES
    half = width // HALVES

    def row_of(px, pz, q):
        return px * share_x + pz * share_z + q

    def half_of(h):
        return slice(h * half, (h + 1) * half)

    def x_copy(k, pz, q, h):
        peer = (x + k) % nx
        return pltpu.make_async_remote_copy(
            src_ref=part.at[row_of(peer, pz, q), :, half_of(h)],
            dst_ref=from_x.at[pz, q, h, k - 1],
            send_sem=send5.at[0],
            recv_sem=recv5.at[pz, q, h],
            device_id={"views": in_x(peer)},
            device_id_type=MESH,
        )

    def place(i, carry):
        pz, q = (zh + 1 + i // share_z) % nz, i % share_z
        for d in [row_of((x + 1 + k) % nx, pz, q) for k in range(nx)]:
            lefts = [None] * (blocks + 2)
            rights = [None] * (blocks + 2)
            for v in range(views):
                start = start_of(v, d)
                block, rest = start >> 7, start & (LANES - 1)
                for ref, sums in ((spread_left, lefts), (spread_right, rights)):
                    turned = ref[v, d, pl.ds(2 - block, blocks + 3)]
                    for j in range(blocks + 2):
                        value = jnp.where(lane >= rest, turned[j + 1], turned[j])
                        sums[j] = value if v == 0 else sums[j] + value

            def total_of(value):
                return jnp.sum(value, axis=1, keepdims=True)

            low_left, low_right = total_of(lefts[0]), total_of(rights[0])
            top = lane == LANES - 1
            high_left = total_of(lefts[-1] + jnp.where(top, lefts[-2], 0.0))
            high_right = total_of(rights[-1])
            shifted = [pltpu.roll(rights[j + 1], 1, 1) for j in range(blocks)]
            for j in range(blocks):
                left = lefts[j + 1]
                if j == 0:
                    right = jnp.where(lane == 0, 0.0, shifted[0])
                    left = left + jnp.where(lane == 0, low_left, 0.0) + jnp.where(lane == 1, low_right, 0.0)
                else:
                    right = jnp.where(lane == 0, shifted[j - 1], shifted[j])
                if j == blocks - 1:
                    left = jnp.where(top, high_right + rights[-2], left)
                    left = left + jnp.where(lane == LANES - 2, high_left, 0.0)
                part[d, :, j * LANES : (j + 1) * LANES] = left + right

        for h in range(HALVES):
            for k in range(1, nx):
                x_copy(k, pz, q, h).start()
        return carry

    lax.fori_loop(0, nz * share_z, place, 0)

    def reduce_x(pz, s):
        q, h = divmod(s, HALVES)
        all_of(from_x.at[pz, q, h], recv5.at[pz, q, h]).wait_recv()
        value = part[row_of(x, pz, q), :, half_of(h)]
        for k in range(1, nx):
            value = value + from_x[pz, q, h, k - 1]
        z_out[pz, s] = value

    def z_copy(peer, s, slot):
        return pltpu.make_async_remote_copy(
            src_ref=z_out.at[peer, s],
            dst_ref=from_z.at[slot, s],
            send_sem=send6.at[0],
            recv_sem=recv6.at[slot, s],
            device_id={"views": in_z(peer)},
            device_id_type=MESH,
        )

    def give(to, px, pz, s, send, recv):
        q, h = divmod(s, HALVES)
        piece = full.at[row_of(px, pz, q), :, half_of(h)]
        return pltpu.make_async_remote_copy(
            src_ref=piece,
            dst_ref=piece,
            send_sem=send,
            recv_sem=recv,
            device_id={"views": to},
            device_id_type=MESH,
        )

    def give_z(peer, px, pz, s):
        return give(in_z(peer), px, pz, s, send8.at[0], recv8.at[pz, s])

    for s in range(pieces):
        for k in range(1, nz):
            reduce_x((zh + k) % nz, s)
            z_copy((zh + k) % nz, s, zh).start()

    def onward(s):
        return 1 if s % 2 == 0 else nx - 1

    def to_relay(px, pz, s):
        return give(in_x((px + onward(s)) % nx), px, pz, s, send7.at[0], recv7.at[pz, s])

    def spread_x(pz, s):
        to_relay(x, pz, s).start()
        give(in_x((x + nx - onward(s)) % nx), x, pz, s, send7.at[0], recv9.at[0]).start()

    def relay(turn, s):
        px, pz = (x + nx - onward(s)) % nx, (zh + turn) % nz
        to_relay(px, pz, s).wait_recv()
        give(in_x((x + onward(s)) % nx), px, pz, s, send7.at[0], recv9.at[1]).start()

    for s in range(pieces):
        reduce_x(zh, s)
        for k in range(1, nz):
            z_copy((zh + k) % nz, s, (zh + k) % nz).wait_recv()
        value = z_out[zh, s]
        for k in range(1, nz):
            value = value + from_z[(zh + k) % nz, s]
        q, h = divmod(s, HALVES)
        full[row_of(x, zh, q), :, half_of(h)] = value
        for k in range(1, nz):
            give_z((zh + k) % nz, x, zh, s).start()
        spread_x(zh, s)
    for s in range(pieces):
        relay(0, s)
        for k in range(1, nz):
            pz = (zh + k) % nz
            give_z(pz, x, pz, s).wait_recv()
            spread_x(pz, s)
    for k in range(1, nz):
        for s in range(pieces):
            relay(k, s)

    def turn_out(px):
        for o in range(share_x // TILE):
            at = pl.ds(pl.multiple_of(px * share_x + o * TILE, TILE), TILE)
            for j in range(blocks):
                columns = slice(j * LANES, (j + 1) * LANES)
                grad[:, at, columns] = jnp.transpose(full[at, :, columns], (1, 0, 2))

    turn_out(x)
    all_of(full.at[:share_x], recv9.at[0]).wait_recv()
    turn_out((x + 1) % nx)
    turn_out((x + nx - 1) % nx)
    all_of(full.at[:share_x], recv9.at[1]).wait_recv()
    turn_out((x + 2) % nx)

    all_of(signal.at[:, : nc - 1], recv4.at[0]).wait_recv()
    all_of(slab.at[: nc - 1], send1.at[0]).wait_send()
    all_of(group_recv.at[: ny - 1], send2.at[0]).wait_send()
    all_of(back.at[: nc - 1], send3.at[0]).wait_send()
    all_of(signal.at[:, : nc - 1], send4.at[0]).wait_send()
    all_of(part.at[: (nx - 1) * share_x], send5.at[0]).wait_send()
    all_of(z_out.at[: nz - 1], send6.at[0]).wait_send()
    all_of(full.at[: (nx - 1) * share_x], send7.at[0]).wait_send()
    all_of(z_out.at[: nz - 1], send8.at[0]).wait_send()


def body(sizes, concentration, shear_index, shear_weight, attenuation, yields, line_energy, measured):
    elements, rows, depth, width = concentration.shape
    views = shear_index.shape[0]
    nx, nz, ny, nc = sizes
    wide = views * width // nc
    tiles = wide // LANES
    blocks = width // LANES
    share_z = depth // nx // nz
    hbm = pl.BlockSpec(memory_space=pltpu.HBM)
    vmem = pl.BlockSpec(memory_space=pltpu.VMEM)
    full = depth * elements

    def buf(*shape):
        return pltpu.VMEM(shape, F32)

    def sems(*shape):
        return pltpu.SemaphoreType.DMA(shape)

    gradient, signal = pl.pallas_call(
        functools.partial(kernel, sizes),
        out_shape=(
            pltpu.VMEM((elements, depth, width), F32),
            pltpu.VMEM((views, elements, rows, width), F32),
        ),
        in_specs=[hbm] * 7,
        out_specs=(vmem, vmem),
        scratch_shapes=[
            pltpu.SMEM((views, depth, LANES), jnp.int32),
            pltpu.SMEM(attenuation.shape, F32),
            pltpu.SMEM(yields.shape, F32),
            pltpu.SMEM(line_energy.shape, jnp.int32),
            buf(elements, depth, width),
            buf(views, depth, width),
            buf(elements, rows, wide),
            sems(7),
        ]
        + [pltpu.VMEM((full, full), BF16)] * 4
        + [buf(depth, blocks + 3, elements, LANES)] * 2
        + [buf(views, full, width)] * 2
        + [buf(views, depth, blocks + 5, elements, LANES)] * 2
        + [
            buf(PAIR, full, STEP),
            buf(nc, tiles + tiles // 2, elements, LANES),
            buf(nc, tiles + tiles // 2, elements, LANES),
            buf(nc, elements, wide),
            buf(nc, elements, wide),
            buf(tiles + tiles // 2, elements, LANES),
            buf(ny, tiles + tiles // 2, elements, LANES),
            buf(ny, elements, wide),
            buf(nc, tiles + tiles // 2, elements, LANES),
            buf(nc, tiles + tiles // 2, elements, LANES),
            buf(elements, rows, wide),
            buf(depth, elements, width),
            buf(nz, share_z, HALVES, nx - 1, elements, width // HALVES),
            buf(nz, share_z * HALVES, elements, width // HALVES),
            buf(nz, share_z * HALVES, elements, width // HALVES),
            buf(depth, elements, width),
        ]
        + [sems(1)] * 5
        + [sems(nc)]
        + [sems(1)] * 3
        + [sems(nz, share_z, HALVES), sems(1), sems(nz, share_z * HALVES)]
        + [sems(1), sems(nz, share_z * HALVES), sems(1), sems(nz, share_z * HALVES), sems(2)],
        compiler_params=pltpu.CompilerParams(
            collective_id=0, has_side_effects=True, vmem_limit_bytes=56 * 1024 * 1024
        ),
    )(
        shear_index,
        attenuation,
        yields,
        line_energy,
        concentration.reshape(elements, depth, width),
        shear_weight,
        measured,
    )
    return gradient.reshape(elements, rows, depth, width), signal


SIZES = {(8, 64): (4, 2, 8, 8)}


def solution(mesh):
    sizes = SIZES[mesh.shape["views"], mesh.shape["depth"]]
    return jax.shard_map(
        functools.partial(body, sizes),
        mesh=mesh,
        in_specs=(
            P(None, None, "depth", None),
            P("views", "depth", None),
            P("views", "depth", None),
            P(),
            P(),
            P(),
            P("views", None, None, None),
        ),
        out_specs=(P(None, None, "depth", None), P("views", None, None, None)),
        check_vma=False,
    )
```

```python
import functools

import jax
import jax.numpy as jnp
from jax import lax
from jax.experimental import pallas as pl
from jax.experimental.pallas import tpu as pltpu
from jax.sharding import PartitionSpec as P

LANES = 128
TILE = 8
STEP = 256
PAIR = 4
HALVES = 1
MESH = pl.DeviceIdType.MESH
F32 = jnp.float32
BF16 = jnp.bfloat16


def split(value):
    high = value.astype(BF16)
    low = (value - high.astype(F32)).astype(BF16)
    return high, low


def dot3(high_ref, low_ref, right):
    right_high, right_low = split(right)
    high = high_ref[...]
    result = jnp.dot(high, right_high, preferred_element_type=F32)
    result += jnp.dot(high, right_low, preferred_element_type=F32)
    return result + jnp.dot(low_ref[...], right_high, preferred_element_type=F32)


def kernel(
    sizes,
    index_in,
    att_in,
    yields_in,
    line_in,
    conc_in,
    weight_in,
    measured_in,
    grad,
    signal,
    shifts,
    att,
    yields,
    line,
    conc,
    weight,
    measured,
    fetched,
    mat_high,
    mat_low,
    adj_high,
    adj_low,
    pad_left,
    pad_step,
    field,
    decay,
    spread_left,
    spread_right,
    corr,
    slab,
    group,
    local_scale,
    local_part,
    group_send,
    group_recv,
    group_scale,
    back,
    seeds,
    total_send,
    part,
    from_x,
    z_out,
    from_z,
    full,
    send1,
    recv1,
    send2,
    recv2,
    send3,
    recv3,
    send4,
    recv4,
    send5,
    recv5,
    send6,
    recv6,
    send7,
    recv7,
    send8,
    recv8,
    recv9,
):
    nx, nz, ny, nc = sizes
    views, depth, width = weight.shape
    blocks = width // LANES
    wide = views * width // nc
    per_view = width // wide
    tiles = wide // LANES
    depth_total = depth * ny * nc
    vi, di = lax.axis_index("views"), lax.axis_index("depth")
    x, zh = vi // nz, vi % nz
    y, c = di // nc, di % nc

    def flip(k):
        bits = [((c // b + k // b) % 2) * b for b in (1, 2, 4) if b < nc]
        return sum(bits)

    def in_group(k):
        return y * nc + k

    def in_y(k):
        return k * nc + c

    def in_x(k):
        return k * nz + zh

    def in_z(k):
        return x * nz + k

    own_view, own_base = c // per_view, pl.multiple_of((c % per_view) * wide, LANES)
    own_at = pl.ds(own_base, wide)
    middle = width // 2
    fetches = [
        pltpu.make_async_copy(src, dst, fetched.at[min(i, 6)])
        for i, (src, dst) in enumerate(
            [
                (conc_in, conc),
                (weight_in, weight),
                (index_in.at[:, :, middle : middle + LANES], shifts),
                (att_in, att),
                (yields_in, yields),
                (line_in, line),
            ]
            + [(measured_in.at[own_view, e, :, own_at], measured.at[e]) for e in range(TILE)]
        )
    ]
    for fetch in fetches:
        fetch.start()

    def start_of(v, d):
        return jnp.clip(shifts[v, d, 0] - (middle - LANES), 0, 2 * LANES)

    def all_of(ref, sem):
        return pltpu.make_async_remote_copy(
            src_ref=ref,
            dst_ref=ref,
            send_sem=sem,
            recv_sem=sem,
            device_id={"depth": in_group(flip(1))},
            device_id_type=MESH,
        )

    barrier = pltpu.get_barrier_semaphore()
    greeted = 0
    for k in range(1, nc):
        pl.semaphore_signal(barrier, inc=1, device_id={"depth": in_group((c + k) % nc)}, device_id_type=MESH)
        greeted += 1
    for k in range(1, ny):
        pl.semaphore_signal(barrier, inc=1, device_id={"depth": in_y((y + k) % ny)}, device_id_type=MESH)
        greeted += 1
    for k in range(1, nx):
        pl.semaphore_signal(barrier, inc=1, device_id={"views": in_x((x + k) % nx)}, device_id_type=MESH)
        greeted += 1
    for k in range(1, nz):
        pl.semaphore_signal(barrier, inc=1, device_id={"views": in_z((zh + k) % nz)}, device_id_type=MESH)
        greeted += 1

    for fetch in fetches[3:6]:
        fetch.wait()

    rows16 = lax.broadcasted_iota(jnp.int32, (2 * TILE, depth * TILE), 0)
    cols16 = lax.broadcasted_iota(jnp.int32, (2 * TILE, depth * TILE), 1)
    row_item, col_item, col_depth = rows16 & (TILE - 1), cols16 & (TILE - 1), cols16 // TILE

    def spread(item, values):
        result = jnp.full(item.shape, values[0])
        for i in range(1, TILE):
            result = jnp.where(item == i, values[i], result)
        return result

    att_col = [spread(col_item, [att[k, e] for e in range(TILE)]) for k in range(4)]
    att_row = [spread(row_item, [att[k, e] for e in range(TILE)]) for k in range(4)]
    line_col = spread(col_item, [line[e] for e in range(TILE)])
    line_row = spread(row_item, [line[e] for e in range(TILE)])

    def pick(which, options):
        return jnp.where(which == 0, options[0], jnp.where(which == 1, options[1], options[2]))

    forward_out = pick(line_row, att_col[1:])
    adjoint_out = pick(line_col, att_row[1:])
    for i in range(depth // 2):
        here = rows16 // TILE + 2 * i
        rows = pl.ds(2 * TILE * i, 2 * TILE)
        mat = jnp.where(col_depth < here, att_col[0], jnp.where(col_depth > here, forward_out, 0.0))
        mat_high[rows, :], mat_low[rows, :] = split(mat)
        adj = jnp.where(col_depth > here, att_row[0], jnp.where(col_depth < here, adjoint_out, 0.0))
        adj_high[rows, :], adj_low[rows, :] = split(adj)
    att_tile = [value[:TILE, :LANES] for value in att_row]
    line_tile = line_row[:TILE, :LANES]
    yield_tile = spread(row_item[:TILE, :LANES], [yields[e] for e in range(TILE)])

    def over(tile, columns):
        return jnp.concatenate([tile] * (columns // LANES), axis=1)

    lane = lax.broadcasted_iota(jnp.int32, (TILE, LANES), 1)
    sub = lax.broadcasted_iota(jnp.int32, (TILE, LANES), 0)

    def stack_rows(levels):
        result = jnp.broadcast_to(levels[0], (TILE, LANES))
        for k in range(1, TILE):
            result = jnp.where(sub == k, jnp.broadcast_to(levels[k], (TILE, LANES)), result)
        return result

    def columns_of(ref, j):
        return jnp.concatenate([ref[j, b] for b in range(tiles)], axis=1)

    def packed_row(ref, j, b, k):
        at = 4 * (b % 2) + k
        return jnp.broadcast_to(ref[j, tiles + b // 2, at : at + 1, :], (TILE, LANES))

    fetches[0].wait()

    def turn_rows(i, carry):
        at = pl.ds(pl.multiple_of(i * TILE, TILE), TILE)
        for j in range(blocks):
            columns = slice(j * LANES, (j + 1) * LANES)
            part[at, :, columns] = jnp.transpose(conc[:, at, columns], (1, 0, 2))
        return carry

    lax.fori_loop(0, depth // TILE, turn_rows, 0, unroll=True)

    def pad_row(d, carry):
        x_blocks = [part[d, :, j * LANES : (j + 1) * LANES] for j in range(blocks)]
        turned = [pltpu.roll(block, LANES - 1, 1) for block in x_blocks]

        def lane_of(block, at):
            return jnp.broadcast_to(block[:, at : at + 1], (TILE, LANES))

        first, second = lane_of(x_blocks[0], 0), lane_of(x_blocks[0], 1)
        before_last, last = lane_of(x_blocks[-1], LANES - 2), lane_of(x_blocks[-1], LANES - 1)
        pad_left[d, 0] = first
        pad_step[d, 0] = second - first
        for j in range(blocks):
            if j < blocks - 1:
                left = x_blocks[j]
                right = jnp.where(lane == LANES - 1, turned[j + 1], turned[j])
            else:
                left = jnp.where(lane == LANES - 1, before_last, x_blocks[j])
                right = jnp.where(lane == LANES - 1, last, turned[j])
            pad_left[d, j + 1] = left
            pad_step[d, j + 1] = right - left
        for j in (blocks + 1, blocks + 2):
            pad_left[d, j] = before_last
            pad_step[d, j] = last - before_last
        return carry

    lax.fori_loop(0, depth, pad_row, 0, unroll=8)

    for fetch in fetches[1:3]:
        fetch.wait()

    for v in range(views):

        def take_row(d, row, shares, sums):
            start = start_of(v, d)
            block, rest = start >> 7, start & (LANES - 1)
            turn = (LANES - rest) & (LANES - 1)
            left = pltpu.roll(pad_left[d, pl.ds(block, blocks + 1)], turn, 2)
            step = pltpu.roll(pad_step[d, pl.ds(block, blocks + 1)], turn, 2)
            whole = lane < LANES - rest
            new = []
            for j in range(blocks):
                at = pl.ds(j * LANES, LANES)
                share = jnp.broadcast_to(shares[row : row + 1, j * LANES : (j + 1) * LANES], (TILE, LANES))
                value = jnp.where(whole, left[j], left[j + 1]) + share * jnp.where(whole, step[j], step[j + 1])
                field[v, pl.ds(pl.multiple_of(d * TILE, TILE), TILE), at] = value
                new.append(sums[j] + value)
            return tuple(new)

        def take_rows(i, sums):
            base = pl.multiple_of(i * TILE, TILE)
            shares = weight[v, pl.ds(base, TILE), :]
            for row in range(TILE):
                sums = take_row(base + row, row, shares, sums)
            return sums

        zero = jnp.zeros((TILE, LANES), F32)
        sums = lax.fori_loop(0, depth // TILE, take_rows, (zero,) * blocks, unroll=2)
        for j in range(0, blocks, 2):
            chunk, offset = divmod(v * blocks + j, tiles)
            levels = [
                jnp.sum(att_tile[k] * sums[j + h], axis=0, keepdims=True) for h in range(2) for k in range(4)
            ]
            slab[chunk, tiles + offset // 2] = stack_rows(levels)

    pl.semaphore_wait(barrier, greeted)

    def to_group(k):
        return pltpu.make_async_remote_copy(
            src_ref=slab.at[k],
            dst_ref=group.at[c],
            send_sem=send1.at[0],
            recv_sem=recv1.at[0],
            device_id={"depth": in_group(k)},
            device_id_type=MESH,
        )

    def emit_chunk(chunk):
        v, base = chunk // per_view, (chunk % per_view) * wide
        for part_at in range(0, wide, STEP):
            at = pl.ds(pl.multiple_of(base + part_at, STEP), STEP)
            values = field[v, :, at]
            value = jnp.exp(-dot3(mat_high, mat_low, values))
            decay[v, :, at] = value
            value = (value * values).reshape(depth, TILE, STEP)
            value = jnp.sum(value, axis=0)
            for j in range(STEP // LANES):
                slab[chunk, part_at // LANES + j] = value[:, j * LANES : (j + 1) * LANES] * yield_tile

    def emit(i, carry):
        chunks = [flip(nc - PAIR * (i + 1) + k) for k in range(PAIR)]
        for chunk in chunks:
            emit_chunk(chunk)
        for chunk in chunks:

            @pl.when(chunk != c)
            def _():
                to_group(chunk).start()

        return carry

    lax.fori_loop(0, nc // PAIR, emit, 0)
    group[c] = slab[c]

    all_of(group.at[: nc - 1], recv1.at[0]).wait_recv()

    line_wide = over(line_tile, wide)

    def scales(ref, count):
        first, later = [], []
        for j in range(count):
            levels = [
                jnp.concatenate([packed_row(ref, j, b, k) for b in range(tiles)], axis=1) for k in range(4)
            ]
            first.append(levels[0])
            later.append(pick(line_wide, levels[1:]))
        after = [None] * count
        run = jnp.zeros((TILE, wide), F32)
        for j in reversed(range(count)):
            after[j] = run
            run = run + later[j]
        result = []
        run = jnp.zeros((TILE, wide), F32)
        for j in range(count):
            result.append(jnp.exp(-(run + after[j])))
            run = run + first[j]
        return result

    emitted_sum = jnp.zeros((TILE, wide), F32)
    for j, scale in enumerate(scales(group, nc)):
        piece = columns_of(group, j) * scale
        local_scale[j] = scale
        local_part[j] = piece
        emitted_sum += piece
    for b in range(tiles):
        group_send[b] = emitted_sum[:, b * LANES : (b + 1) * LANES]
    for b in range(tiles, tiles + tiles // 2):
        value = group[0, b]
        for j in range(1, nc):
            value = value + group[j, b]
        group_send[b] = value

    def y_copy(peer, slot):
        return pltpu.make_async_remote_copy(
            src_ref=group_send,
            dst_ref=group_recv.at[slot],
            send_sem=send2.at[0],
            recv_sem=recv2.at[0],
            device_id={"depth": in_y(peer)},
            device_id_type=MESH,
        )

    for k in sorted(range(1, ny), key=lambda k: -min(k, ny - k)):
        y_copy((y + k) % ny, y).start()
    group_recv[y] = group_send[...]
    all_of(group_recv.at[: ny - 1], recv2.at[0]).wait_recv()

    total = jnp.zeros((TILE, wide), F32)
    prior = jnp.zeros((TILE, wide), F32)
    following = jnp.zeros((TILE, wide), F32)
    for j, scale in enumerate(scales(group_recv, ny)):
        piece = columns_of(group_recv, j) * scale
        group_scale[j] = scale
        total += piece
        prior += jnp.where(j < y, piece, 0.0)
        following += jnp.where(j > y, piece, 0.0)
    pltpu.make_async_copy(measured, measured, fetched.at[6]).wait()
    counts = total * (1.0 / depth_total)
    misfit = counts - jnp.concatenate([measured[e] for e in range(TILE)], axis=0)
    here_scale = group_scale[y]
    later = [None] * nc
    run = following
    for j in reversed(range(nc)):
        later[j] = jnp.sum(misfit * run, axis=0, keepdims=True)
        run = run + local_part[j] * here_scale
    run = prior
    yield_wide = over(yield_tile, wide)
    for j in range(nc):
        value = misfit * yield_wide * local_scale[j] * here_scale
        for b in range(tiles):
            back[j, b] = value[:, b * LANES : (b + 1) * LANES]
        mixed = misfit * run
        levels = [later[j]] + [
            jnp.sum(jnp.where(line_wide == k, mixed, 0.0), axis=0, keepdims=True) for k in range(3)
        ]
        for b in range(0, tiles, 2):
            back[j, tiles + b // 2] = stack_rows(
                [level[:, (b + h) * LANES : (b + h + 1) * LANES] for h in range(2) for level in levels]
            )
        run = run + local_part[j] * here_scale

    def seed_copy(peer, slot):
        return pltpu.make_async_remote_copy(
            src_ref=back.at[peer],
            dst_ref=seeds.at[slot],
            send_sem=send3.at[0],
            recv_sem=recv3.at[slot],
            device_id={"depth": in_group(peer)},
            device_id_type=MESH,
        )

    def total_copy(peer, slot):
        at = pl.ds(pl.multiple_of((slot % per_view) * wide, LANES), wide)
        return pltpu.make_async_remote_copy(
            src_ref=total_send,
            dst_ref=signal.at[slot // per_view, :, :, at],
            send_sem=send4.at[0],
            recv_sem=recv4.at[0],
            device_id={"depth": in_group(peer)},
            device_id_type=MESH,
        )

    for k in reversed(range(1, nc)):
        seed_copy(flip(k), c).start()
    seeds[c] = back[c]
    for e in range(TILE):
        total_send[e] = counts[e : e + 1]
        signal[own_view, e, :, own_at] = counts[e : e + 1]

    def clear(d, carry):
        zeros = jnp.zeros((3, TILE, LANES), F32)
        for v in range(views):
            spread_left[v, d, 0:3] = zeros
            spread_right[v, d, 0:3] = zeros
            spread_left[v, d, 3 + blocks : 5 + blocks] = zeros[:2]
            spread_right[v, d, 3 + blocks : 5 + blocks] = zeros[:2]
        return carry

    lax.fori_loop(0, depth, clear, 0)

    def adjoint_chunk(chunk, corr):
        v, base = chunk // per_view, (chunk % per_view) * wide
        for part_at in range(0, wide, STEP):
            start = pl.multiple_of(base + part_at, STEP)
            at = pl.ds(start, STEP)
            here = range(part_at // LANES, (part_at + STEP) // LANES)
            factor = jnp.concatenate([seeds[chunk, b] for b in here], axis=1)
            constant = jnp.concatenate(
                [sum(att_tile[k] * packed_row(seeds, chunk, b, k) for k in range(4)) for b in here], axis=1
            )
            direct = decay[v, :, at].reshape(depth, TILE, STEP) * factor[None]
            mixed = direct.reshape(depth * TILE, STEP) * field[v, :, at]
            corr[...] = dot3(adj_high, adj_low, mixed)
            for d in range(depth):
                if d % TILE == 0:
                    shares = weight[v, d : d + TILE, at]
                rows = slice(d * TILE, (d + 1) * TILE)
                value = decay[v, rows, at] * factor - corr[rows, :] - constant
                right = value * jnp.broadcast_to(shares[d % TILE : d % TILE + 1], (TILE, STEP))
                left = value - right
                rest = start_of(v, d) & (LANES - 1)
                for j in range(STEP // LANES):
                    to = 3 + start // LANES + j
                    spread_left[v, d, to] = pltpu.roll(left[:, j * LANES : (j + 1) * LANES], rest, 1)
                    spread_right[v, d, to] = pltpu.roll(right[:, j * LANES : (j + 1) * LANES], rest, 1)

    def adjoint(i, carry):
        chunks = [flip(PAIR * i + k) for k in range(PAIR)]
        for chunk in chunks:

            @pl.when(chunk != c)
            def _():
                seed_copy(chunk, chunk).wait_recv()

        for k, chunk in enumerate(chunks):
            adjoint_chunk(chunk, corr.at[k])
        return carry

    lax.fori_loop(0, nc // PAIR, adjoint, 0)

    for k in range(1, nc):
        total_copy((c + k) % nc, c).start()
    share_x = depth // nx
    share_z = share_x // nz
    pieces = share_z * HALVES
    half = width // HALVES

    def row_of(px, pz, q):
        return px * share_x + pz * share_z + q

    def half_of(h):
        return slice(h * half, (h + 1) * half)

    def x_copy(k, pz, q, h):
        peer = (x + k) % nx
        return pltpu.make_async_remote_copy(
            src_ref=part.at[row_of(peer, pz, q), :, half_of(h)],
            dst_ref=from_x.at[pz, q, h, k - 1],
            send_sem=send5.at[0],
            recv_sem=recv5.at[pz, q, h],
            device_id={"views": in_x(peer)},
            device_id_type=MESH,
        )

    def place(i, carry):
        pz, q = (zh + 1 + i // share_z) % nz, i % share_z
        for d in [row_of((x + 1 + k) % nx, pz, q) for k in range(nx)]:
            lefts = [None] * (blocks + 2)
            rights = [None] * (blocks + 2)
            for v in range(views):
                start = start_of(v, d)
                block, rest = start >> 7, start & (LANES - 1)
                for ref, sums in ((spread_left, lefts), (spread_right, rights)):
                    turned = ref[v, d, pl.ds(2 - block, blocks + 3)]
                    for j in range(blocks + 2):
                        value = jnp.where(lane >= rest, turned[j + 1], turned[j])
                        sums[j] = value if v == 0 else sums[j] + value

            def total_of(value):
                return jnp.sum(value, axis=1, keepdims=True)

            low_left, low_right = total_of(lefts[0]), total_of(rights[0])
            top = lane == LANES - 1
            high_left = total_of(lefts[-1] + jnp.where(top, lefts[-2], 0.0))
            high_right = total_of(rights[-1])
            shifted = [pltpu.roll(rights[j + 1], 1, 1) for j in range(blocks)]
            for j in range(blocks):
                left = lefts[j + 1]
                if j == 0:
                    right = jnp.where(lane == 0, 0.0, shifted[0])
                    left = left + jnp.where(lane == 0, low_left, 0.0) + jnp.where(lane == 1, low_right, 0.0)
                else:
                    right = jnp.where(lane == 0, shifted[j - 1], shifted[j])
                if j == blocks - 1:
                    left = jnp.where(top, high_right + rights[-2], left)
                    left = left + jnp.where(lane == LANES - 2, high_left, 0.0)
                part[d, :, j * LANES : (j + 1) * LANES] = left + right

        for h in range(HALVES):
            for k in range(1, nx):
                x_copy(k, pz, q, h).start()
        return carry

    lax.fori_loop(0, nz * share_z, place, 0)

    def reduce_x(pz, s):
        q, h = divmod(s, HALVES)
        all_of(from_x.at[pz, q, h], recv5.at[pz, q, h]).wait_recv()
        value = part[row_of(x, pz, q), :, half_of(h)]
        for k in range(1, nx):
            value = value + from_x[pz, q, h, k - 1]
        z_out[pz, s] = value

    def z_copy(peer, s, slot):
        return pltpu.make_async_remote_copy(
            src_ref=z_out.at[peer, s],
            dst_ref=from_z.at[slot, s],
            send_sem=send6.at[0],
            recv_sem=recv6.at[slot, s],
            device_id={"views": in_z(peer)},
            device_id_type=MESH,
        )

    def give(to, px, pz, s, send, recv):
        q, h = divmod(s, HALVES)
        piece = full.at[row_of(px, pz, q), :, half_of(h)]
        return pltpu.make_async_remote_copy(
            src_ref=piece,
            dst_ref=piece,
            send_sem=send,
            recv_sem=recv,
            device_id={"views": to},
            device_id_type=MESH,
        )

    def give_z(peer, px, pz, s):
        return give(in_z(peer), px, pz, s, send8.at[0], recv8.at[pz, s])

    for s in range(pieces):
        for k in range(1, nz):
            reduce_x((zh + k) % nz, s)
            z_copy((zh + k) % nz, s, zh).start()

    def onward(s):
        return 1 if s % 2 == 0 else nx - 1

    def to_relay(px, pz, s):
        return give(in_x((px + onward(s)) % nx), px, pz, s, send7.at[0], recv7.at[pz, s])

    def spread_x(pz, s):
        to_relay(x, pz, s).start()
        give(in_x((x + nx - onward(s)) % nx), x, pz, s, send7.at[0], recv9.at[0]).start()

    def relay(turn, s):
        px, pz = (x + nx - onward(s)) % nx, (zh + turn) % nz
        to_relay(px, pz, s).wait_recv()
        give(in_x((x + onward(s)) % nx), px, pz, s, send7.at[0], recv9.at[1]).start()

    for s in range(pieces):
        reduce_x(zh, s)
        for k in range(1, nz):
            z_copy((zh + k) % nz, s, (zh + k) % nz).wait_recv()
        value = z_out[zh, s]
        for k in range(1, nz):
            value = value + from_z[(zh + k) % nz, s]
        q, h = divmod(s, HALVES)
        full[row_of(x, zh, q), :, half_of(h)] = value
        for k in range(1, nz):
            give_z((zh + k) % nz, x, zh, s).start()
        spread_x(zh, s)
    for s in range(pieces):
        relay(0, s)
        for k in range(1, nz):
            pz = (zh + k) % nz
            give_z(pz, x, pz, s).wait_recv()
            spread_x(pz, s)
    for k in range(1, nz):
        for s in range(pieces):
            relay(k, s)

    def turn_out(px):
        for o in range(share_x // TILE):
            at = pl.ds(pl.multiple_of(px * share_x + o * TILE, TILE), TILE)
            for j in range(blocks):
                columns = slice(j * LANES, (j + 1) * LANES)
                grad[:, at, columns] = jnp.transpose(full[at, :, columns], (1, 0, 2))

    turn_out(x)
    all_of(full.at[:share_x], recv9.at[0]).wait_recv()
    turn_out((x + 1) % nx)
    turn_out((x + nx - 1) % nx)
    all_of(full.at[:share_x], recv9.at[1]).wait_recv()
    turn_out((x + 2) % nx)

    all_of(signal.at[:, : nc - 1], recv4.at[0]).wait_recv()
    all_of(slab.at[: nc - 1], send1.at[0]).wait_send()
    all_of(group_recv.at[: ny - 1], send2.at[0]).wait_send()
    all_of(back.at[: nc - 1], send3.at[0]).wait_send()
    all_of(signal.at[:, : nc - 1], send4.at[0]).wait_send()
    all_of(part.at[: (nx - 1) * share_x], send5.at[0]).wait_send()
    all_of(z_out.at[: nz - 1], send6.at[0]).wait_send()
    all_of(full.at[: (nx - 1) * share_x], send7.at[0]).wait_send()
    all_of(z_out.at[: nz - 1], send8.at[0]).wait_send()


def body(sizes, concentration, shear_index, shear_weight, attenuation, yields, line_energy, measured):
    elements, rows, depth, width = concentration.shape
    views = shear_index.shape[0]
    nx, nz, ny, nc = sizes
    wide = views * width // nc
    tiles = wide // LANES
    blocks = width // LANES
    share_z = depth // nx // nz
    hbm = pl.BlockSpec(memory_space=pltpu.HBM)
    vmem = pl.BlockSpec(memory_space=pltpu.VMEM)
    full = depth * elements

    def buf(*shape):
        return pltpu.VMEM(shape, F32)

    def sems(*shape):
        return pltpu.SemaphoreType.DMA(shape)

    gradient, signal = pl.pallas_call(
        functools.partial(kernel, sizes),
        out_shape=(
            pltpu.VMEM((elements, depth, width), F32),
            pltpu.VMEM((views, elements, rows, width), F32),
        ),
        in_specs=[hbm] * 7,
        out_specs=(vmem, vmem),
        scratch_shapes=[
            pltpu.SMEM((views, depth, LANES), jnp.int32),
            pltpu.SMEM(attenuation.shape, F32),
            pltpu.SMEM(yields.shape, F32),
            pltpu.SMEM(line_energy.shape, jnp.int32),
            buf(elements, depth, width),
            buf(views, depth, width),
            buf(elements, rows, wide),
            sems(7),
        ]
        + [pltpu.VMEM((full, full), BF16)] * 4
        + [buf(depth, blocks + 3, elements, LANES)] * 2
        + [buf(views, full, width)] * 2
        + [buf(views, depth, blocks + 5, elements, LANES)] * 2
        + [
            buf(PAIR, full, STEP),
            buf(nc, tiles + tiles // 2, elements, LANES),
            buf(nc, tiles + tiles // 2, elements, LANES),
            buf(nc, elements, wide),
            buf(nc, elements, wide),
            buf(tiles + tiles // 2, elements, LANES),
            buf(ny, tiles + tiles // 2, elements, LANES),
            buf(ny, elements, wide),
            buf(nc, tiles + tiles // 2, elements, LANES),
            buf(nc, tiles + tiles // 2, elements, LANES),
            buf(elements, rows, wide),
            buf(depth, elements, width),
            buf(nz, share_z, HALVES, nx - 1, elements, width // HALVES),
            buf(nz, share_z * HALVES, elements, width // HALVES),
            buf(nz, share_z * HALVES, elements, width // HALVES),
            buf(depth, elements, width),
        ]
        + [sems(1)] * 5
        + [sems(nc)]
        + [sems(1)] * 3
        + [sems(nz, share_z, HALVES), sems(1), sems(nz, share_z * HALVES)]
        + [sems(1), sems(nz, share_z * HALVES), sems(1), sems(nz, share_z * HALVES), sems(2)],
        compiler_params=pltpu.CompilerParams(
            collective_id=0, has_side_effects=True, vmem_limit_bytes=56 * 1024 * 1024
        ),
    )(
        shear_index,
        attenuation,
        yields,
        line_energy,
        concentration.reshape(elements, depth, width),
        shear_weight,
        measured,
    )
    return gradient.reshape(elements, rows, depth, width), signal


SIZES = {(8, 64): (4, 2, 8, 8)}


def solution(mesh):
    sizes = SIZES[mesh.shape["views"], mesh.shape["depth"]]
    return jax.shard_map(
        functools.partial(body, sizes),
        mesh=mesh,
        in_specs=(
            P(None, None, "depth", None),
            P("views", "depth", None),
            P("views", "depth", None),
            P(),
            P(),
            P(),
            P("views", None, None, None),
        ),
        out_specs=(P(None, None, "depth", None), P("views", None, None, None)),
        check_vma=False,
    )
```
